1024 devices in a mesh: node: 128 (over x, z), feat: 8 (over y, core).
Axes of the slice: x: 4, y: 4, z: 32, core: 2. Of those that a mesh axis runs over, the one named last changes fastest.
Arguments:
- features: bfloat16 [256, 524288], P('feat', 'node'), may hold values from -6 to 6
- weight_one: bfloat16 [256, 256], replicated, may hold values from -0.375 to 0.375
- weight_two: bfloat16 [256, 256], replicated, may hold values from -0.375 to 0.375
- blk_rows: int32 [128, 128], P('node'), may hold values from 0 to 31, as said below
- blk_cols: int32 [128, 128], P('node'), may hold values from 0 to 4095, as said below
- blk_counts: int32 [128], P('node'), may hold values from 32 to 128, as said below
- adj_values: bfloat16 [16384, 128, 128], P('node')
- adj_tvalues: bfloat16 [16384, 128, 128], P('node'), as said below
- cotangent: bfloat16 [256, 524288], P('feat', 'node'), may hold values from -0.0078125 to 0.0078125
Outputs:
- hidden_out: bfloat16 [256, 524288], P('feat', 'node')
- grad_one: float32 [256, 256], replicated
- grad_two: float32 [256, 256], replicated
The draws below stay inside these ranges and needn't reach their ends.
Inputs may be any that keep to these rules, and one draw needn't show every extreme that they name: `blk_rows`: slots m >= blk_counts[s] of shard s are unused and hold 0. `blk_cols`: for shard s a live slot's block column lies in shards s - 1, s or s + 1; no (row, column) block repeats among a shard's live slots; the set of live blocks of the whole matrix is symmetric; at most 16 live slots of a shard have their column in shard s + 1, and at most 16 in shard s - 1, and some shard reaches this bound on each side; unused slots hold s * 32. `blk_counts`: every shard's 32 diagonal blocks are live; some shard uses all 128 slots. `adj_tvalues`: each live slot holds the transpose of the adj_values block at the mirrored block position, so B is the transpose of A.
All inputs are finite; a program needn't handle non-finite values.
Results may differ from the reference program's by a relative error of at most 0.015.
Values may be sent and summed in bfloat16 or wider, within the bound.
No kernel may reach another device: no remote copies, remote signals or barrier semaphores. Data moves between devices by JAX's collectives and lax.ppermute only.
A program may use at most 64 MiB of HBM per device.

```python
import jax
import jax.numpy as jnp
import numpy as np
from jax import lax

D = 256
BLK = 128
NBD = 32
MAXB = 128
SHARDS = 128
NBLK = 4096
NODES = 524288


def block_layout(key):
    shards = NBLK // NBD
    key_cross, key_level, key_busy, key_inner, key_pairs, key_order = jax.random.split(key, 6)
    boundary = jnp.arange(shards + 1)
    cross_pairs = 2 * jax.random.randint(key_cross, (shards + 1,), 1, NBD // 4 + 1)
    cross_pairs = jnp.where(boundary == 1, NBD // 2, cross_pairs)
    cross_pairs = jnp.where((boundary > 0) & (boundary < shards), cross_pairs, 0)
    left_cross = cross_pairs[:shards]
    right_cross = cross_pairs[1:]
    capacity = (MAXB - NBD - left_cross - right_cross) // 2
    load_level = jax.random.randint(key_level, (shards,), 0, 9)
    inner_pairs = capacity * load_level * load_level // 64
    busiest = jax.random.randint(key_busy, (), 0, shards)
    inner_pairs = jnp.where(jnp.arange(shards) == busiest, capacity, inner_pairs)
    upper_i, upper_j = np.triu_indices(NBD, 1)
    upper_i = jnp.asarray(upper_i, jnp.int32)
    upper_j = jnp.asarray(upper_j, jnp.int32)
    inner_total = upper_i.shape[0]
    inner_rank = jax.vmap(lambda seed_key: jnp.argsort(jax.random.permutation(seed_key, inner_total)))(jax.random.split(key_inner, shards))
    inner_live = inner_rank < inner_pairs[:, None]
    cross_rank = jax.vmap(lambda seed_key: jnp.argsort(jax.random.permutation(seed_key, NBD * NBD)))(jax.random.split(key_pairs, shards + 1))
    cross_live = cross_rank < cross_pairs[:, None]
    cross_i = jnp.arange(NBD * NBD) // NBD
    cross_j = jnp.arange(NBD * NBD) % NBD
    own_base = jnp.arange(shards)[:, None] * NBD
    diagonal = jnp.arange(NBD)
    rows_all = jnp.concatenate([diagonal, upper_i, upper_j, cross_j, cross_i])
    rows_all = jnp.broadcast_to(rows_all[None, :], (shards, rows_all.shape[0]))
    cols_all = jnp.concatenate([own_base + diagonal[None, :], own_base + upper_j[None, :], own_base + upper_i[None, :], own_base - NBD + cross_i[None, :], own_base + NBD + cross_j[None, :]], axis=1)
    live_all = jnp.concatenate([jnp.ones((shards, NBD), bool), inner_live, inner_live, cross_live[:shards], cross_live[1:]], axis=1)
    candidates = rows_all.shape[1]
    shuffled = jax.vmap(lambda seed_key: jax.random.permutation(seed_key, candidates))(jax.random.split(key_order, shards))
    dead_flags = 1 - jnp.take_along_axis(live_all, shuffled, axis=1).astype(jnp.int32)
    sorted_order = jnp.argsort(dead_flags, axis=1, stable=True)
    chosen = jnp.take_along_axis(shuffled, sorted_order, axis=1)[:, :MAXB]
    counts = NBD + 2 * inner_pairs + left_cross + right_cross
    in_use = jnp.arange(MAXB)[None, :] < counts[:, None]
    block_rows = jnp.where(in_use, jnp.take_along_axis(rows_all, chosen, axis=1), 0)
    block_cols = jnp.where(in_use, jnp.take_along_axis(cols_all, chosen, axis=1), own_base)
    return (block_rows.astype(jnp.int32), block_cols.astype(jnp.int32), counts.astype(jnp.int32))


def pair_keys(block_rows, block_cols, mirrored):
    shards = NBLK // NBD
    global_rows = jnp.arange(shards)[:, None] * NBD + block_rows
    if mirrored:
        return (block_cols * NBLK + global_rows).reshape(-1)
    return (global_rows * NBLK + block_cols).reshape(-1)


def draw_blk_rows(key, part):
    return block_layout(key)[0]


def draw_blk_cols(key, part):
    return block_layout(key)[1]


def draw_blk_counts(key, part):
    return block_layout(key)[2]


def draw_adj_values(key, part):
    block_rows, block_cols, counts = block_layout(key)
    value_key = jax.random.fold_in(key, 7)
    keys_used = pair_keys(block_rows, block_cols, False)
    blocks = jax.vmap(lambda pair_key: jax.random.normal(jax.random.fold_in(value_key, pair_key), (BLK, BLK), jnp.float32))(keys_used)
    return (blocks * (3.0 * BLK) ** (-0.5)).astype(jnp.bfloat16)


def draw_adj_tvalues(key, part):
    block_rows, block_cols, counts = block_layout(key)
    value_key = jax.random.fold_in(key, 7)
    keys_used = pair_keys(block_rows, block_cols, True)
    blocks = jax.vmap(lambda pair_key: jax.random.normal(jax.random.fold_in(value_key, pair_key), (BLK, BLK), jnp.float32))(keys_used)
    blocks = jnp.transpose(blocks, (0, 2, 1))
    return (blocks * (3.0 * BLK) ** (-0.5)).astype(jnp.bfloat16)


def level_of(own_key, extent, cuts, smallest, top_value):
    factor_of, own = 1.0, jax.random.fold_in(own_key, 6)
    for axis_at, blocks in cuts:
        steps = jnp.exp(jax.random.uniform(jax.random.fold_in(own, axis_at), (blocks,), jnp.float32, smallest / len(cuts), top_value / len(cuts)))
        factor_of = factor_of * jnp.repeat(steps, extent[axis_at] // blocks).reshape([-1 if axis == axis_at else 1 for axis in range(len(extent))])
    return factor_of


def gaussian(rng, dims, spread, bound, cuts=(), held_as=jnp.bfloat16):
    factor_of = level_of(rng, dims, cuts, -0.22, 0.18) if cuts else 1.0
    array = jax.random.normal(rng, dims, jnp.float32) * spread * factor_of
    return jnp.minimum(jnp.maximum(array, -bound), bound).astype(held_as)


def setup_inputs(seed: int = 0) -> dict:
    splits = jax.random.split(jax.random.key(seed), 10)
    return {
        "features": gaussian(splits[0], (D, NODES), 1.0, 6.0, ((0, 8), (1, 128))),
        "weight_one": gaussian(splits[1], (D, D), D ** -0.5, 0.375),
        "weight_two": gaussian(splits[2], (D, D), D ** -0.5, 0.375),
        "blk_rows": draw_blk_rows(jax.random.fold_in(splits[9], 71), 0),
        "blk_cols": draw_blk_cols(jax.random.fold_in(splits[9], 71), 0),
        "blk_counts": draw_blk_counts(jax.random.fold_in(splits[9], 71), 0),
        "adj_values": draw_adj_values(jax.random.fold_in(splits[9], 71), 0),
        "adj_tvalues": draw_adj_tvalues(jax.random.fold_in(splits[9], 71), 0),
        "cotangent": gaussian(splits[8], (D, NODES), (NODES ** -0.5), 0.0078125, ((0, 8), (1, 128))),
    }


def silu_grad(values):
    sigma = jax.nn.sigmoid(values)
    return sigma * (1.0 + values * (1.0 - sigma))

def apply_blocks(source, row_ids, col_ids, live_totals, adj_blocks):
    grouped = source.reshape(source.shape[0], NBLK, BLK)
    shaped = adj_blocks.reshape(SHARDS, MAXB, BLK, BLK)
    slot_ids = jnp.arange(MAXB).astype(jnp.int32)
    target = jnp.arange(NBD).astype(jnp.int32)

    def per_shard(shard_item):
        shard_rows, shard_cols, live_total, shard_blocks = shard_item
        picked = jnp.take(grouped, shard_cols, axis=1).astype(jnp.float32)
        partial_value = jnp.einsum('fmk,mjk->fmj', picked, shard_blocks.astype(jnp.float32))
        chooser = ((shard_rows[:, None] == target[None, :]) & (slot_ids < live_total)[:, None]).astype(jnp.float32)
        return jnp.einsum('mr,fmj->frj', chooser, partial_value, precision=lax.Precision.HIGHEST)
    stacked = lax.map(per_shard, (row_ids, col_ids, live_totals, shaped))
    return jnp.transpose(stacked, (1, 0, 2, 3)).reshape(source.shape[0], NODES)

def reference(features, weight_one, weight_two, blk_rows, blk_cols, blk_counts, adj_values, adj_tvalues, cotangent):
    proj_one = jnp.dot(weight_one.T, features, preferred_element_type=jnp.float32).astype(jnp.bfloat16)
    pre_one = apply_blocks(proj_one, blk_rows, blk_cols, blk_counts, adj_values)
    hidden_one = jax.nn.silu(pre_one).astype(jnp.bfloat16)
    proj_two = jnp.dot(weight_two.T, hidden_one, preferred_element_type=jnp.float32).astype(jnp.bfloat16)
    pre_two = apply_blocks(proj_two, blk_rows, blk_cols, blk_counts, adj_values)
    hidden_out = jax.nn.silu(pre_two).astype(jnp.bfloat16)
    delta_two = (cotangent.astype(jnp.float32) * silu_grad(pre_two)).astype(jnp.bfloat16)
    back_two = apply_blocks(delta_two, blk_rows, blk_cols, blk_counts, adj_tvalues).astype(jnp.bfloat16)
    grad_two = jnp.dot(hidden_one, back_two.T, preferred_element_type=jnp.float32)
    carry_one = jnp.dot(weight_two, back_two, preferred_element_type=jnp.float32).astype(jnp.bfloat16)
    delta_one = (carry_one.astype(jnp.float32) * silu_grad(pre_one)).astype(jnp.bfloat16)
    back_one = apply_blocks(delta_one, blk_rows, blk_cols, blk_counts, adj_tvalues).astype(jnp.bfloat16)
    grad_one = jnp.dot(features, back_one.T, preferred_element_type=jnp.float32)
    return (hidden_out, grad_one, grad_two)
```

```python
import jax
import jax.numpy as jnp
import numpy as np
from jax import lax
from jax.experimental import pallas as pl
from jax.experimental.pallas import tpu as pltpu
from jax.sharding import Mesh, PartitionSpec as P

BLK = 128
NBD = 32
HALO = 16
GROUPS = 8
PER_GROUP = NBD // GROUPS
FEATS = 32
SLOTS_PER_STEP = 16
BF16 = jnp.bfloat16
F32 = jnp.float32

FINE = {"x": 4, "zhi": 8, "zlo": 4, "y": 4, "core": 2}
NODE = ("x", "zhi", "zlo")
FEAT = ("y", "core")
PLANE = ("x", "y", "core")

SMEM = pl.BlockSpec(memory_space=pltpu.SMEM)
VMEM = pl.BlockSpec(memory_space=pltpu.VMEM)


def blocks_of(dtype=BF16):
    return jax.ShapeDtypeStruct((NBD, FEATS, BLK), dtype)


def halo_blocks():
    return jax.ShapeDtypeStruct((HALO, FEATS, BLK), BF16)


def exchange(array, axes):
    return lax.all_to_all(array, axes, split_axis=0, concat_axis=0, tiled=True)


def halo(send_low, send_high):
    count = lax.axis_size(NODE)
    forward = [(i, i + 1) for i in range(count - 1)]
    backward = [(target, source) for source, target in forward]
    low = lax.ppermute(send_high, NODE, forward)
    high = lax.ppermute(send_low, NODE, backward)
    return low, high


def slot_tables(rows, cols, count, position):
    slot = jnp.arange(rows.shape[0])
    live = slot < count
    local = cols - position * NBD
    side = jnp.where(live & (local < 0), 1, jnp.where(live & (local >= NBD), 2, 0))
    same = side[:, None] == side[None, :]
    send_key = rows * (4 * NBD) + local + NBD
    recv_key = (local + NBD) * (4 * NBD) + rows
    send_rank = jnp.sum(same & (send_key[None, :] < send_key[:, None]), axis=1)
    recv_rank = jnp.sum(same & (recv_key[None, :] < recv_key[:, None]), axis=1)
    place = jnp.where(side > 0, (side - 1) * HALO + send_rank, 4 * HALO)
    hit = place[None, :] == jnp.arange(2 * HALO)[:, None]
    send = jnp.sum(jnp.where(hit, rows[None, :], 0), axis=1)
    own = jnp.where(live, HALO + local, HALO)
    source = jnp.where(side == 1, recv_rank, jnp.where(side == 2, HALO + NBD + recv_rank, own))
    target = jnp.where(live, rows, NBD)
    return send.astype(jnp.int32), source.astype(jnp.int32), target.astype(jnp.int32)


def sigmoid(values):
    return 1.0 / (1.0 + jnp.exp(-values))


def gather_sends(send, blocks, low, high):
    for k in range(HALO):
        low[k] = blocks[send[k]]
        high[k] = blocks[send[HALO + k]]


def split_kernel(send, source, blocks, low, high):
    for b in range(NBD):
        blocks[b] = source[:, b * BLK : (b + 1) * BLK]
    gather_sends(send, blocks, low, high)


def split_blocks(send, source):
    return pl.pallas_call(
        split_kernel,
        in_specs=[SMEM, VMEM],
        out_specs=[VMEM] * 3,
        out_shape=[blocks_of(), halo_blocks(), halo_blocks()],
        name="split_blocks",
    )(send, source)


def sends_kernel(send, blocks, low, high):
    gather_sends(send, blocks, low, high)


def sends_of(send, blocks):
    return pl.pallas_call(
        sends_kernel,
        in_specs=[SMEM, VMEM],
        out_specs=[VMEM] * 2,
        out_shape=[halo_blocks(), halo_blocks()],
        name="sends_of",
    )(send, blocks)


def apply_kernel(source, target, low, own, high, adj, out, held, total):
    step = pl.program_id(0)

    @pl.when(step == 0)
    def _():
        held[0:HALO] = low[...]
        held[HALO : HALO + NBD] = own[...]
        held[HALO + NBD :] = high[...]
        total[...] = jnp.zeros_like(total)

    for j in range(SLOTS_PER_STEP):
        m = step * SLOTS_PER_STEP + j
        part = lax.dot_general(
            held[source[m]], adj[j], (((1,), (1,)), ((), ())), preferred_element_type=F32
        )
        row = target[m]
        total[row] = total[row] + part

    @pl.when(step == pl.num_programs(0) - 1)
    def _():
        out[...] = total[0:NBD].astype(BF16)


def apply_blocks(tables, low, own, high, adj):
    slots = adj.shape[0]
    whole = lambda count: pl.BlockSpec((count, FEATS, BLK), lambda i, *_: (0, 0, 0))
    return pl.pallas_call(
        apply_kernel,
        grid_spec=pltpu.PrefetchScalarGridSpec(
            num_scalar_prefetch=2,
            grid=(slots // SLOTS_PER_STEP,),
            in_specs=[
                whole(HALO),
                whole(NBD),
                whole(HALO),
                pl.BlockSpec((SLOTS_PER_STEP, BLK, BLK), lambda i, *_: (i, 0, 0)),
            ],
            out_specs=whole(NBD),
            scratch_shapes=[
                pltpu.VMEM((2 * HALO + NBD, FEATS, BLK), BF16),
                pltpu.VMEM((NBD + 1, FEATS, BLK), F32),
            ],
        ),
        out_shape=blocks_of(),
        name="apply_blocks",
    )(*tables, low, own, high, adj)


def rows_of(ref):
    parts = []
    for b in range(PER_GROUP):
        parts.append(
            jnp.concatenate([ref[g * PER_GROUP + b] for g in range(GROUPS)], axis=0)
        )
    return jnp.concatenate(parts, axis=1)


def put_rows(ref, values):
    for g in range(GROUPS):
        for b in range(PER_GROUP):
            ref[g * PER_GROUP + b] = values[
                g * FEATS : (g + 1) * FEATS, b * BLK : (b + 1) * BLK
            ]


def mix_one_kernel(spread, weight, hidden, slope):
    pre = lax.dot_general(
        weight[...], rows_of(spread), (((0,), (0,)), ((), ())), preferred_element_type=F32
    )
    sigma = sigmoid(pre)
    put_rows(hidden, (pre * sigma).astype(BF16))
    slope[...] = sigma * (1.0 + pre * (1.0 - sigma))


def mix_one(spread, weight):
    shape = (GROUPS * FEATS, PER_GROUP * BLK)
    return pl.pallas_call(
        mix_one_kernel,
        in_specs=[VMEM] * 2,
        out_specs=[VMEM] * 2,
        out_shape=[blocks_of(), jax.ShapeDtypeStruct(shape, F32)],
        name="mix_one",
    )(spread, weight)


def mix_two_kernel(spread, weight, pre_two):
    pre = lax.dot_general(
        weight[...], rows_of(spread), (((0,), (0,)), ((), ())), preferred_element_type=F32
    )
    put_rows(pre_two, pre.astype(BF16))


def mix_two(spread, weight):
    return pl.pallas_call(
        mix_two_kernel,
        in_specs=[VMEM] * 2,
        out_specs=VMEM,
        out_shape=blocks_of(),
        name="mix_two",
    )(spread, weight)


def turn_kernel(send, pre_two, cotangent, hidden_out, delta, low, high):
    for b in range(NBD):
        span = slice(b * BLK, (b + 1) * BLK)
        pre = pre_two[b].astype(F32)
        sigma = sigmoid(pre)
        hidden_out[:, span] = (pre * sigma).astype(BF16)
        slope = sigma * (1.0 + pre * (1.0 - sigma))
        delta[b] = (cotangent[:, span].astype(F32) * slope).astype(BF16)
    gather_sends(send, delta, low, high)


def turn(send, pre_two, cotangent):
    return pl.pallas_call(
        turn_kernel,
        in_specs=[SMEM, VMEM, VMEM],
        out_specs=[VMEM] * 4,
        out_shape=[
            jax.ShapeDtypeStruct(cotangent.shape, BF16),
            blocks_of(),
            halo_blocks(),
            halo_blocks(),
        ],
        name="turn",
    )(send, pre_two, cotangent)


def grads_kernel(back_two, spread_one, hidden_one, slope, weight, out):
    back = rows_of(back_two)
    along = (((1,), (1,)), ((), ()))
    carry = jnp.dot(weight[...], back, preferred_element_type=F32).astype(BF16)
    delta = (carry.astype(F32) * slope[...]).astype(BF16)
    size = GROUPS * FEATS
    grad_one = lax.dot_general(rows_of(spread_one), delta, along, preferred_element_type=F32)
    grad_two = lax.dot_general(rows_of(hidden_one), back, along, preferred_element_type=F32)
    out[0:size] = grad_one.astype(out.dtype)
    out[size:] = grad_two.astype(out.dtype)


def grads(back_two, spread_one, hidden_one, slope, weight):
    size = GROUPS * FEATS
    return pl.pallas_call(
        grads_kernel,
        in_specs=[VMEM] * 5,
        out_specs=VMEM,
        out_shape=jax.ShapeDtypeStruct((2 * size, size), BF16),
        name="grads",
    )(back_two, spread_one, hidden_one, slope, weight)


def gather_pieces(piece, axes):
    spread = jnp.broadcast_to(piece[None], (lax.axis_size(axes),) + piece.shape)
    return exchange(spread, axes)


def sum_everywhere(partial):
    pieces = exchange(partial.reshape(lax.axis_size(PLANE), -1, BLK), PLANE)
    piece = jnp.sum(pieces.astype(F32), axis=0)
    piece = jnp.sum(gather_pieces(piece, "zlo"), axis=0).astype(BF16)
    piece = jnp.sum(gather_pieces(piece, "zhi").astype(F32), axis=0).astype(BF16)
    return gather_pieces(piece, PLANE).reshape(partial.shape).astype(F32)


def shards(
    features,
    weight_one,
    weight_two,
    blk_rows,
    blk_cols,
    blk_counts,
    adj_values,
    adj_tvalues,
    cotangent,
):
    position = lax.axis_index(NODE)
    send, source, target = slot_tables(
        blk_rows.reshape(-1), blk_cols.reshape(-1), blk_counts[0], position
    )
    tables = (source, target)
    own, low, high = split_blocks(send, features)
    low, high = halo(low, high)
    spread_one = exchange(apply_blocks(tables, low, own, high, adj_values), FEAT)
    hidden_rows, slope_one = mix_one(spread_one, weight_one)
    own = exchange(hidden_rows, FEAT)
    low, high = halo(*sends_of(send, own))
    spread_two = exchange(apply_blocks(tables, low, own, high, adj_values), FEAT)
    pre_two = exchange(mix_two(spread_two, weight_two), FEAT)
    hidden_out, delta_two, low, high = turn(send, pre_two, cotangent)
    low, high = halo(low, high)
    back_two = exchange(apply_blocks(tables, low, delta_two, high, adj_tvalues), FEAT)
    total = sum_everywhere(grads(back_two, spread_one, hidden_rows, slope_one, weight_two))
    size = weight_one.shape[0]
    return (hidden_out, total[:size], total[size:])


def solution(mesh):
    fine = Mesh(np.asarray(mesh.devices).reshape(tuple(FINE.values())), tuple(FINE))
    return jax.shard_map(
        shards,
        mesh=fine,
        in_specs=(
            P(FEAT, NODE),
            P(),
            P(),
            P(NODE, None),
            P(NODE, None),
            P(NODE),
            P(NODE, None, None),
            P(NODE, None, None),
            P(FEAT, NODE),
        ),
        out_specs=(P(FEAT, NODE), P(), P()),
        check_vma=False,
    )
```

```python
import jax
import jax.numpy as jnp
import numpy as np
from jax import lax
from jax.experimental import pallas as pl
from jax.experimental.pallas import tpu as pltpu
from jax.sharding import Mesh, PartitionSpec as P

BLK = 128
NBD = 32
HALO = 16
GROUPS = 8
PER_GROUP = NBD // GROUPS
FEATS = 32
BATCH = 8
SIDE_KEY = 16384.0
BF16 = jnp.bfloat16
F32 = jnp.float32

FINE = {"x": 4, "zhi": 8, "zlo": 4, "y": 4, "core": 2}
NODE = ("x", "zhi", "zlo")
FEAT = ("y", "core")
PLANE = ("x", "y", "core")

SMEM = pl.BlockSpec(memory_space=pltpu.SMEM)
VMEM = pl.BlockSpec(memory_space=pltpu.VMEM)
PARAMS = pltpu.CompilerParams(vmem_limit_bytes=16 * 2**20)


def blocks_of(dtype=BF16):
    return jax.ShapeDtypeStruct((NBD, FEATS, BLK), dtype)


def halo_blocks():
    return jax.ShapeDtypeStruct((HALO, FEATS, BLK), BF16)


def exchange(array, axes):
    return lax.all_to_all(array, axes, split_axis=0, concat_axis=0, tiled=True)


def halo(send_low, send_high):
    count = lax.axis_size(NODE)
    forward = [(i, i + 1) for i in range(count - 1)]
    backward = [(target, source) for source, target in forward]
    low = lax.ppermute(send_high, NODE, forward)
    high = lax.ppermute(send_low, NODE, backward)
    return low, high


def turned(row):
    return jnp.transpose(jnp.broadcast_to(row, (BLK, row.shape[1])))


def rank(key, side):
    before = turned(key)
    earlier = (before < key) & (before >= side * SIDE_KEY)
    return jnp.sum(jnp.where(earlier, 1.0, 0.0), axis=0, keepdims=True)


def slot_tables(rows, cols, count, base):
    slot = lax.broadcasted_iota(jnp.int32, rows.shape, 1)
    live = slot < count
    local = (cols - base).astype(F32)
    rows = rows.astype(F32)
    low = live & (local < 0.0)
    high = live & (local >= float(NBD))
    side = jnp.where(low, 1.0, jnp.where(high, 2.0, 0.0))
    offset = side * SIDE_KEY
    shifted = local + float(NBD)
    send_rank = rank(offset + rows * BLK + shifted, side)
    recv_rank = rank(offset + shifted * BLK + rows, side)
    place = jnp.where(side > 0.0, (side - 1.0) * HALO + send_rank, float(BLK))
    lane = lax.broadcasted_iota(jnp.int32, (BLK, BLK), 1).astype(F32)
    send = jnp.sum(jnp.where(turned(place) == lane, turned(rows), 0.0), axis=0, keepdims=True)
    own = jnp.where(live, HALO + local, float(HALO))
    source = jnp.where(low, recv_rank, jnp.where(high, HALO + NBD + recv_rank, own))
    target = jnp.where(live, rows, float(NBD))
    return send.astype(jnp.int32), source.astype(jnp.int32), target.astype(jnp.int32)


def sigmoid(values):
    return 1.0 / (1.0 + jnp.exp(-values))


def gather_sends(tables, blocks, low, high):
    for k in range(HALO):
        low[k] = blocks[tables[0, k]]
        high[k] = blocks[tables[0, HALO + k]]


def split_kernel(scalars, rows, cols, source, tables, blocks, low, high, scalar_tables, done):
    found = slot_tables(rows[...], cols[...], scalars[0], scalars[1])
    tables[...] = jnp.zeros_like(tables)
    for place, table in enumerate(found):
        tables[place : place + 1] = table
    copy = pltpu.make_async_copy(tables, scalar_tables, done)
    copy.start()
    for b in range(NBD):
        blocks[b] = source[:, b * BLK : (b + 1) * BLK]
    copy.wait()
    gather_sends(scalar_tables, blocks, low, high)


def split_blocks(scalars, rows, cols, source):
    return pl.pallas_call(
        split_kernel,
        in_specs=[SMEM, VMEM, VMEM, VMEM],
        out_specs=[VMEM] * 4,
        out_shape=[
            jax.ShapeDtypeStruct((8, BLK), jnp.int32),
            blocks_of(),
            halo_blocks(),
            halo_blocks(),
        ],
        scratch_shapes=[pltpu.SMEM((8, BLK), jnp.int32), pltpu.SemaphoreType.DMA],
        compiler_params=PARAMS,
        name="split_blocks",
    )(scalars, rows, cols, source)


def sends_kernel(tables, blocks, low, high):
    gather_sends(tables, blocks, low, high)


def sends_of(tables, blocks):
    return pl.pallas_call(
        sends_kernel,
        in_specs=[SMEM, VMEM],
        out_specs=[VMEM] * 2,
        out_shape=[halo_blocks(), halo_blocks()],
        compiler_params=PARAMS,
        name="sends_of",
    )(tables, blocks)


def apply_kernel(tables, low, own, high, adj, out, held, total):
    held[0:HALO] = low[...]
    held[HALO : HALO + NBD] = own[...]
    held[HALO + NBD :] = high[...]
    total[...] = jnp.zeros_like(total)
    for start in range(0, adj.shape[0], BATCH):
        slots = range(start, start + BATCH)
        parts = [
            lax.dot_general(
                held[tables[1, m]], adj[m], (((1,), (1,)), ((), ())), preferred_element_type=F32
            )
            for m in slots
        ]
        for m, part in zip(slots, parts):
            row = tables[2, m]
            total[row] = total[row] + part
    out[...] = total[0:NBD].astype(BF16)


def apply_blocks(tables, low, own, high, adj):
    return pl.pallas_call(
        apply_kernel,
        in_specs=[SMEM] + [VMEM] * 4,
        out_specs=VMEM,
        out_shape=blocks_of(),
        scratch_shapes=[
            pltpu.VMEM((2 * HALO + NBD, FEATS, BLK), BF16),
            pltpu.VMEM((NBD + 1, FEATS, BLK), F32),
        ],
        compiler_params=PARAMS,
        name="apply_blocks",
    )(tables, low, own, high, adj)


def rows_of(ref):
    parts = []
    for b in range(PER_GROUP):
        parts.append(
            jnp.concatenate([ref[g * PER_GROUP + b] for g in range(GROUPS)], axis=0)
        )
    return jnp.concatenate(parts, axis=1)


def put_rows(ref, values):
    for g in range(GROUPS):
        for b in range(PER_GROUP):
            ref[g * PER_GROUP + b] = values[
                g * FEATS : (g + 1) * FEATS, b * BLK : (b + 1) * BLK
            ]


def mix_one_kernel(spread, weight, hidden, slope):
    pre = lax.dot_general(
        weight[...], rows_of(spread), (((0,), (0,)), ((), ())), preferred_element_type=F32
    )
    sigma = sigmoid(pre)
    put_rows(hidden, (pre * sigma).astype(BF16))
    slope[...] = sigma * (1.0 + pre * (1.0 - sigma))


def mix_one(spread, weight):
    shape = (GROUPS * FEATS, PER_GROUP * BLK)
    return pl.pallas_call(
        mix_one_kernel,
        in_specs=[VMEM] * 2,
        out_specs=[VMEM] * 2,
        out_shape=[blocks_of(), jax.ShapeDtypeStruct(shape, F32)],
        compiler_params=PARAMS,
        name="mix_one",
    )(spread, weight)


def mix_two_kernel(spread, weight, pre_two):
    pre = lax.dot_general(
        weight[...], rows_of(spread), (((0,), (0,)), ((), ())), preferred_element_type=F32
    )
    put_rows(pre_two, pre.astype(BF16))


def mix_two(spread, weight):
    return pl.pallas_call(
        mix_two_kernel,
        in_specs=[VMEM] * 2,
        out_specs=VMEM,
        out_shape=blocks_of(),
        compiler_params=PARAMS,
        name="mix_two",
    )(spread, weight)


def turn_kernel(tables, pre_two, cotangent, hidden_out, delta, low, high):
    for b in range(NBD):
        span = slice(b * BLK, (b + 1) * BLK)
        pre = pre_two[b].astype(F32)
        sigma = sigmoid(pre)
        hidden_out[:, span] = (pre * sigma).astype(BF16)
        slope = sigma * (1.0 + pre * (1.0 - sigma))
        delta[b] = (cotangent[:, span].astype(F32) * slope).astype(BF16)
    gather_sends(tables, delta, low, high)


def turn(tables, pre_two, cotangent):
    return pl.pallas_call(
        turn_kernel,
        in_specs=[SMEM, VMEM, VMEM],
        out_specs=[VMEM] * 4,
        out_shape=[
            jax.ShapeDtypeStruct(cotangent.shape, BF16),
            blocks_of(),
            halo_blocks(),
            halo_blocks(),
        ],
        compiler_params=PARAMS,
        name="turn",
    )(tables, pre_two, cotangent)


def piece_places():
    for grad in range(2):
        for half in range(2):
            for part in range(GROUPS):
                place = (2 * grad + half) * GROUPS + part
                yield place, grad, slice(part * FEATS, (part + 1) * FEATS), slice(
                    half * BLK, (half + 1) * BLK
                )


def grads_kernel(back_two, spread_one, hidden_one, slope, weight, out):
    back = rows_of(back_two)
    along = (((1,), (1,)), ((), ()))
    carry = jnp.dot(weight[...], back, preferred_element_type=F32).astype(BF16)
    delta = (carry.astype(F32) * slope[...]).astype(BF16)
    sums = (
        lax.dot_general(rows_of(spread_one), delta, along, preferred_element_type=F32),
        lax.dot_general(rows_of(hidden_one), back, along, preferred_element_type=F32),
    )
    for place, grad, rows, columns in piece_places():
        out[place] = sums[grad][rows, columns].astype(BF16)


def grads(back_two, spread_one, hidden_one, slope, weight):
    return pl.pallas_call(
        grads_kernel,
        in_specs=[VMEM] * 5,
        out_specs=VMEM,
        out_shape=blocks_of(),
        compiler_params=PARAMS,
        name="grads",
    )(back_two, spread_one, hidden_one, slope, weight)


def finish_kernel(pieces, grad_one, grad_two):
    outs = (grad_one, grad_two)
    for place, grad, rows, columns in piece_places():
        outs[grad][rows, columns] = pieces[place].astype(F32)


def finish(pieces):
    size = GROUPS * FEATS
    return pl.pallas_call(
        finish_kernel,
        in_specs=[VMEM],
        out_specs=[VMEM] * 2,
        out_shape=[jax.ShapeDtypeStruct((size, size), F32)] * 2,
        compiler_params=PARAMS,
        name="finish",
    )(pieces)


def gather_pieces(piece, axes):
    spread = jnp.broadcast_to(piece[None], (lax.axis_size(axes),) + piece.shape)
    return exchange(spread, axes)


def sum_everywhere(partial):
    pieces = exchange(partial, PLANE).reshape(lax.axis_size(PLANE), -1, BLK)
    piece = jnp.sum(pieces.astype(F32), axis=0)
    piece = jnp.sum(gather_pieces(piece, "zlo"), axis=0).astype(BF16)
    piece = jnp.sum(gather_pieces(piece, "zhi").astype(F32), axis=0).astype(BF16)
    return gather_pieces(piece, PLANE).reshape(partial.shape)


def shards(
    features,
    weight_one,
    weight_two,
    blk_rows,
    blk_cols,
    blk_counts,
    adj_values,
    adj_tvalues,
    cotangent,
):
    base = lax.axis_index(NODE).astype(jnp.int32) * NBD
    scalars = jnp.stack([blk_counts[0], base])
    tables, own, low, high = split_blocks(scalars, blk_rows, blk_cols, features)
    low, high = halo(low, high)
    spread_one = exchange(apply_blocks(tables, low, own, high, adj_values), FEAT)
    hidden_rows, slope_one = mix_one(spread_one, weight_one)
    own = exchange(hidden_rows, FEAT)
    low, high = halo(*sends_of(tables, own))
    spread_two = exchange(apply_blocks(tables, low, own, high, adj_values), FEAT)
    pre_two = exchange(mix_two(spread_two, weight_two), FEAT)
    hidden_out, delta_two, low, high = turn(tables, pre_two, cotangent)
    low, high = halo(low, high)
    back_two = exchange(apply_blocks(tables, low, delta_two, high, adj_tvalues), FEAT)
    partial = grads(back_two, spread_one, hidden_rows, slope_one, weight_two)
    grad_one, grad_two = finish(sum_everywhere(partial))
    return (hidden_out, grad_one, grad_two)


def solution(mesh):
    fine = Mesh(np.asarray(mesh.devices).reshape(tuple(FINE.values())), tuple(FINE))
    return jax.shard_map(
        shards,
        mesh=fine,
        in_specs=(
            P(FEAT, NODE),
            P(),
            P(),
            P(NODE, None),
            P(NODE, None),
            P(NODE),
            P(NODE, None, None),
            P(NODE, None, None),
            P(FEAT, NODE),
        ),
        out_specs=(P(FEAT, NODE), P(), P()),
        check_vma=False,
    )
```

```python
import jax
import jax.numpy as jnp
import numpy as np
from jax import lax
from jax.experimental import pallas as pl
from jax.experimental.pallas import tpu as pltpu
from jax.sharding import Mesh, PartitionSpec as P

BLK = 128
NBD = 32
HALO = 16
GROUPS = 8
PER_GROUP = NBD // GROUPS
FEATS = 32
BATCH = 8
SIDE_KEY = 16384.0
BF16 = jnp.bfloat16
F32 = jnp.float32

FINE = {"x": 4, "zhi": 8, "zlo": 4, "y": 4, "core": 2}
NODE = ("x", "zhi", "zlo")
FEAT = ("y", "core")
PLANE = ("x", "y", "core")

SMEM = pl.BlockSpec(memory_space=pltpu.SMEM)
VMEM = pl.BlockSpec(memory_space=pltpu.VMEM)
PARAMS = pltpu.CompilerParams(vmem_limit_bytes=16 * 2**20)


def blocks_of(dtype=BF16):
    return jax.ShapeDtypeStruct((NBD, FEATS, BLK), dtype)


def halo_blocks():
    return jax.ShapeDtypeStruct((HALO, FEATS, BLK), BF16)


def exchange(array, axes):
    return lax.all_to_all(array, axes, split_axis=0, concat_axis=0, tiled=True)


def halo(send_low, send_high):
    count = lax.axis_size(NODE)
    forward = [(i, i + 1) for i in range(count - 1)]
    backward = [(target, source) for source, target in forward]
    low = lax.ppermute(send_high, NODE, forward)
    high = lax.ppermute(send_low, NODE, backward)
    return low, high


def turned(row):
    return jnp.transpose(jnp.broadcast_to(row, (BLK, row.shape[1])))


def rank(key, side):
    before = turned(key)
    earlier = (before < key) & (before >= side * SIDE_KEY)
    return jnp.sum(jnp.where(earlier, 1.0, 0.0), axis=0, keepdims=True)


def slot_tables(rows, cols, count, base):
    slot = lax.broadcasted_iota(jnp.int32, rows.shape, 1)
    live = slot < count
    local = (cols - base).astype(F32)
    rows = rows.astype(F32)
    low = live & (local < 0.0)
    high = live & (local >= float(NBD))
    side = jnp.where(low, 1.0, jnp.where(high, 2.0, 0.0))
    offset = side * SIDE_KEY
    shifted = local + float(NBD)
    send_rank = rank(offset + rows * BLK + shifted, side)
    recv_rank = rank(offset + shifted * BLK + rows, side)
    first = jnp.where(side > 0.0, (side - 1.0) * HALO, float(BLK))
    lane = lax.broadcasted_iota(jnp.int32, (BLK, BLK), 1).astype(F32)
    slots = lax.broadcasted_iota(jnp.int32, (BLK, BLK), 0).astype(F32)
    rows_down = turned(rows)
    sent = turned(first + send_rank) == lane
    received = turned(first + recv_rank) == lane
    total = lambda hit, values: jnp.sum(jnp.where(hit, values, 0.0), axis=0, keepdims=True)
    own = live & (side == 0.0)
    found = (
        total(sent, rows_down),
        jnp.where(own, local, 0.0),
        jnp.where(own, rows, float(NBD)),
        total(received, slots),
        NBD + total(received, rows_down - NBD),
    )
    return [table.astype(jnp.int32) for table in found]


def sigmoid(values):
    return 1.0 / (1.0 + jnp.exp(-values))


def gather_sends(tables, blocks, low, high):
    for k in range(HALO):
        low[k] = blocks[tables[0, k]]
        high[k] = blocks[tables[0, HALO + k]]


def split_kernel(slots, source, tables, blocks, low, high, scalar_tables, done):
    found = slot_tables(slots[0:1], slots[1:2], slots[2:3], slots[3:4])
    tables[...] = jnp.zeros_like(tables)
    for place, table in enumerate(found):
        tables[place : place + 1] = table
    copy = pltpu.make_async_copy(tables, scalar_tables, done)
    copy.start()
    for b in range(NBD):
        blocks[b] = source[:, b * BLK : (b + 1) * BLK]
    copy.wait()
    gather_sends(scalar_tables, blocks, low, high)


def split_blocks(slots, source):
    return pl.pallas_call(
        split_kernel,
        in_specs=[VMEM] * 2,
        out_specs=[VMEM] * 4,
        out_shape=[
            jax.ShapeDtypeStruct((8, BLK), jnp.int32),
            blocks_of(),
            halo_blocks(),
            halo_blocks(),
        ],
        scratch_shapes=[pltpu.SMEM((8, BLK), jnp.int32), pltpu.SemaphoreType.DMA],
        compiler_params=PARAMS,
        name="split_blocks",
    )(slots, source)


def sends_kernel(tables, blocks, low, high):
    gather_sends(tables, blocks, low, high)


def sends_of(tables, blocks):
    return pl.pallas_call(
        sends_kernel,
        in_specs=[SMEM, VMEM],
        out_specs=[VMEM] * 2,
        out_shape=[halo_blocks(), halo_blocks()],
        compiler_params=PARAMS,
        name="sends_of",
    )(tables, blocks)


def add_slots(total, batch):
    parts = [
        lax.dot_general(block, adj, (((1,), (1,)), ((), ())), preferred_element_type=F32)
        for block, adj, _ in batch
    ]
    for part, (_, _, row) in zip(parts, batch):
        total[row] = total[row] + part


def apply_own_kernel(tables, own, adj, total):
    total[...] = jnp.zeros_like(total)
    for start in range(0, adj.shape[0], BATCH):
        slots = range(start, start + BATCH)
        add_slots(total, [(own[tables[1, m]], adj[m], tables[2, m]) for m in slots])


def apply_own(tables, own, adj):
    return pl.pallas_call(
        apply_own_kernel,
        in_specs=[SMEM] + [VMEM] * 2,
        out_specs=VMEM,
        out_shape=jax.ShapeDtypeStruct((NBD + 1, FEATS, BLK), F32),
        compiler_params=PARAMS,
        name="apply_own",
    )(tables, own, adj)


def apply_halo_kernel(tables, begun, low, high, adj, out, total):
    total[...] = begun[...]
    for side, blocks in enumerate((low, high)):
        for start in range(0, HALO, BATCH):
            batch = []
            for k in range(start, start + BATCH):
                place = side * HALO + k
                batch.append((blocks[k], adj[tables[3, place]], tables[4, place]))
            add_slots(total, batch)
    out[...] = total[0:NBD].astype(BF16)


def apply_halo(tables, begun, low, high, adj):
    return pl.pallas_call(
        apply_halo_kernel,
        in_specs=[SMEM] + [VMEM] * 4,
        out_specs=VMEM,
        out_shape=blocks_of(),
        scratch_shapes=[pltpu.VMEM((NBD + 1, FEATS, BLK), F32)],
        compiler_params=PARAMS,
        name="apply_halo",
    )(tables, begun, low, high, adj)


def apply_blocks(tables, own, sends, adj):
    low, high = halo(*sends)
    return apply_halo(tables, apply_own(tables, own, adj), low, high, adj)


def rows_of(ref):
    parts = []
    for b in range(PER_GROUP):
        parts.append(
            jnp.concatenate([ref[g * PER_GROUP + b] for g in range(GROUPS)], axis=0)
        )
    return jnp.concatenate(parts, axis=1)


def put_rows(ref, values):
    for g in range(GROUPS):
        for b in range(PER_GROUP):
            ref[g * PER_GROUP + b] = values[
                g * FEATS : (g + 1) * FEATS, b * BLK : (b + 1) * BLK
            ]


def mix_one_kernel(spread, weight, hidden, slope):
    pre = lax.dot_general(
        weight[...], rows_of(spread), (((0,), (0,)), ((), ())), preferred_element_type=F32
    )
    sigma = sigmoid(pre)
    put_rows(hidden, (pre * sigma).astype(BF16))
    slope[...] = sigma * (1.0 + pre * (1.0 - sigma))


def mix_one(spread, weight):
    shape = (GROUPS * FEATS, PER_GROUP * BLK)
    return pl.pallas_call(
        mix_one_kernel,
        in_specs=[VMEM] * 2,
        out_specs=[VMEM] * 2,
        out_shape=[blocks_of(), jax.ShapeDtypeStruct(shape, F32)],
        compiler_params=PARAMS,
        name="mix_one",
    )(spread, weight)


def mix_two_kernel(spread, weight, pre_two):
    pre = lax.dot_general(
        weight[...], rows_of(spread), (((0,), (0,)), ((), ())), preferred_element_type=F32
    )
    put_rows(pre_two, pre.astype(BF16))


def mix_two(spread, weight):
    return pl.pallas_call(
        mix_two_kernel,
        in_specs=[VMEM] * 2,
        out_specs=VMEM,
        out_shape=blocks_of(),
        compiler_params=PARAMS,
        name="mix_two",
    )(spread, weight)


def turn_kernel(tables, pre_two, cotangent, delta, low, high):
    for b in range(NBD):
        pre = pre_two[b].astype(F32)
        sigma = sigmoid(pre)
        slope = sigma * (1.0 + pre * (1.0 - sigma))
        span = slice(b * BLK, (b + 1) * BLK)
        delta[b] = (cotangent[:, span].astype(F32) * slope).astype(BF16)
    gather_sends(tables, delta, low, high)


def turn(tables, pre_two, cotangent):
    return pl.pallas_call(
        turn_kernel,
        in_specs=[SMEM, VMEM, VMEM],
        out_specs=[VMEM] * 3,
        out_shape=[blocks_of(), halo_blocks(), halo_blocks()],
        compiler_params=PARAMS,
        name="turn",
    )(tables, pre_two, cotangent)


def hidden_kernel(pre_two, hidden_out):
    for b in range(NBD):
        pre = pre_two[b].astype(F32)
        hidden_out[:, b * BLK : (b + 1) * BLK] = (pre * sigmoid(pre)).astype(BF16)


def hidden_of(pre_two):
    return pl.pallas_call(
        hidden_kernel,
        in_specs=[VMEM],
        out_specs=VMEM,
        out_shape=jax.ShapeDtypeStruct((FEATS, NBD * BLK), BF16),
        compiler_params=PARAMS,
        name="hidden_of",
    )(pre_two)


def piece_places():
    for grad in range(2):
        for half in range(2):
            for part in range(GROUPS):
                place = (2 * grad + half) * GROUPS + part
                yield place, grad, slice(part * FEATS, (part + 1) * FEATS), slice(
                    half * BLK, (half + 1) * BLK
                )


def grads_kernel(back_two, spread_one, hidden_one, slope, weight, out):
    back = rows_of(back_two)
    along = (((1,), (1,)), ((), ()))
    carry = jnp.dot(weight[...], back, preferred_element_type=F32).astype(BF16)
    delta = (carry.astype(F32) * slope[...]).astype(BF16)
    sums = (
        lax.dot_general(rows_of(spread_one), delta, along, preferred_element_type=F32),
        lax.dot_general(rows_of(hidden_one), back, along, preferred_element_type=F32),
    )
    for place, grad, rows, columns in piece_places():
        out[place] = sums[grad][rows, columns].astype(BF16)


def grads(back_two, spread_one, hidden_one, slope, weight):
    return pl.pallas_call(
        grads_kernel,
        in_specs=[VMEM] * 5,
        out_specs=VMEM,
        out_shape=blocks_of(),
        compiler_params=PARAMS,
        name="grads",
    )(back_two, spread_one, hidden_one, slope, weight)


def finish_kernel(pieces, grad_one, grad_two):
    outs = (grad_one, grad_two)
    for place, grad, rows, columns in piece_places():
        outs[grad][rows, columns] = pieces[place].astype(F32)


def finish(pieces):
    size = GROUPS * FEATS
    return pl.pallas_call(
        finish_kernel,
        in_specs=[VMEM],
        out_specs=[VMEM] * 2,
        out_shape=[jax.ShapeDtypeStruct((size, size), F32)] * 2,
        compiler_params=PARAMS,
        name="finish",
    )(pieces)


def gather_pieces(piece, axes):
    spread = jnp.broadcast_to(piece[None], (lax.axis_size(axes),) + piece.shape)
    return exchange(spread, axes)


def sum_everywhere(partial):
    pieces = exchange(partial, PLANE).reshape(lax.axis_size(PLANE), -1, BLK)
    piece = jnp.sum(pieces.astype(F32), axis=0)
    piece = jnp.sum(gather_pieces(piece, "zlo"), axis=0).astype(BF16)
    piece = jnp.sum(gather_pieces(piece, "zhi").astype(F32), axis=0).astype(BF16)
    return gather_pieces(piece, PLANE).reshape(partial.shape)


def shards(
    features,
    weight_one,
    weight_two,
    blk_rows,
    blk_cols,
    blk_counts,
    adj_values,
    adj_tvalues,
    cotangent,
):
    base = lax.axis_index(NODE).astype(jnp.int32) * NBD
    spread = lambda scalar: jnp.broadcast_to(scalar, blk_rows.shape)
    slots = jnp.concatenate([blk_rows, blk_cols, spread(blk_counts[0]), spread(base)])
    tables, own, *sends = split_blocks(slots, features)
    spread_one = exchange(apply_blocks(tables, own, sends, adj_values), FEAT)
    hidden_rows, slope_one = mix_one(spread_one, weight_one)
    own = exchange(hidden_rows, FEAT)
    spread_two = exchange(apply_blocks(tables, own, sends_of(tables, own), adj_values), FEAT)
    pre_two = exchange(mix_two(spread_two, weight_two), FEAT)
    delta_two, *sends = turn(tables, pre_two, cotangent)
    back_two = exchange(apply_blocks(tables, delta_two, sends, adj_tvalues), FEAT)
    hidden_out = hidden_of(pre_two)
    partial = grads(back_two, spread_one, hidden_rows, slope_one, weight_two)
    grad_one, grad_two = finish(sum_everywhere(partial))
    return (hidden_out, grad_one, grad_two)


def solution(mesh):
    fine = Mesh(np.asarray(mesh.devices).reshape(tuple(FINE.values())), tuple(FINE))
    return jax.shard_map(
        shards,
        mesh=fine,
        in_specs=(
            P(FEAT, NODE),
            P(),
            P(),
            P(NODE, None),
            P(NODE, None),
            P(NODE),
            P(NODE, None, None),
            P(NODE, None, None),
            P(FEAT, NODE),
        ),
        out_specs=(P(FEAT, NODE), P(), P()),
        check_vma=False,
    )
```

```python
import jax
import jax.numpy as jnp
import numpy as np
from jax import lax
from jax.experimental import pallas as pl
from jax.experimental.pallas import tpu as pltpu
from jax.sharding import Mesh, PartitionSpec as P

BLK = 128
NBD = 32
HALO = 16
GROUPS = 8
PER_GROUP = NBD // GROUPS
FEATS = 32
BATCH = 8
SIDE_KEY = 16384.0
BF16 = jnp.bfloat16
F32 = jnp.float32

FINE = {"x": 4, "zhi": 8, "zlo": 4, "y": 4, "core": 2}
NODE = ("x", "zhi", "zlo")
FEAT = ("y", "core")
PLANE = ("x", "y", "core")

SMEM = pl.BlockSpec(memory_space=pltpu.SMEM)
VMEM = pl.BlockSpec(memory_space=pltpu.VMEM)
PARAMS = pltpu.CompilerParams(vmem_limit_bytes=16 * 2**20)


def blocks_of(dtype=BF16):
    return jax.ShapeDtypeStruct((NBD, FEATS, BLK), dtype)


def halo_blocks():
    return jax.ShapeDtypeStruct((HALO, FEATS, BLK), BF16)


def exchange(array, axes):
    return lax.all_to_all(array, axes, split_axis=0, concat_axis=0, tiled=True)


def halo(send_low, send_high):
    count = lax.axis_size(NODE)
    forward = [(i, i + 1) for i in range(count - 1)]
    backward = [(target, source) for source, target in forward]
    low = lax.ppermute(send_high, NODE, forward)
    high = lax.ppermute(send_low, NODE, backward)
    return low, high


def turned(row):
    return jnp.transpose(jnp.broadcast_to(row, (BLK, row.shape[1])))


def rank(key, side):
    before = turned(key)
    earlier = (before < key) & (before >= side * SIDE_KEY)
    return jnp.sum(jnp.where(earlier, 1.0, 0.0), axis=0, keepdims=True)


def slot_tables(rows, cols, count, base):
    slot = lax.broadcasted_iota(jnp.int32, rows.shape, 1)
    live = slot < count
    local = (cols - base).astype(F32)
    rows = rows.astype(F32)
    low = live & (local < 0.0)
    high = live & (local >= float(NBD))
    side = jnp.where(low, 1.0, jnp.where(high, 2.0, 0.0))
    offset = side * SIDE_KEY
    shifted = local + float(NBD)
    send_rank = rank(offset + rows * BLK + shifted, side)
    recv_rank = rank(offset + shifted * BLK + rows, side)
    first = jnp.where(side > 0.0, (side - 1.0) * HALO, float(BLK))
    lane = lax.broadcasted_iota(jnp.int32, (BLK, BLK), 1).astype(F32)
    slots = lax.broadcasted_iota(jnp.int32, (BLK, BLK), 0).astype(F32)
    rows_down = turned(rows)
    sent = turned(first + send_rank) == lane
    received = turned(first + recv_rank) == lane
    total = lambda hit, values: jnp.sum(jnp.where(hit, values, 0.0), axis=0, keepdims=True)
    own = live & (side == 0.0)
    found = (
        total(sent, rows_down),
        jnp.where(own, local, 0.0),
        jnp.where(own, rows, float(NBD)),
        total(received, slots),
        NBD + total(received, rows_down - NBD),
    )
    return [table.astype(jnp.int32) for table in found]


def sigmoid(values):
    return 1.0 / (1.0 + jnp.exp(-values))


def gather_sends(tables, blocks, low, high):
    for k in range(HALO):
        low[k] = blocks[tables[0, k]]
        high[k] = blocks[tables[0, HALO + k]]


def split_kernel(slots, source, tables, blocks, low, high, scalar_tables, done):
    found = slot_tables(slots[0:1], slots[1:2], slots[2:3], slots[3:4])
    tables[...] = jnp.zeros_like(tables)
    for place, table in enumerate(found):
        tables[place : place + 1] = table
    copy = pltpu.make_async_copy(tables, scalar_tables, done)
    copy.start()
    for b in range(NBD):
        blocks[b] = source[:, b * BLK : (b + 1) * BLK]
    copy.wait()
    gather_sends(scalar_tables, blocks, low, high)


def split_blocks(slots, source):
    return pl.pallas_call(
        split_kernel,
        in_specs=[VMEM] * 2,
        out_specs=[VMEM] * 4,
        out_shape=[
            jax.ShapeDtypeStruct((8, BLK), jnp.int32),
            blocks_of(),
            halo_blocks(),
            halo_blocks(),
        ],
        scratch_shapes=[pltpu.SMEM((8, BLK), jnp.int32), pltpu.SemaphoreType.DMA],
        compiler_params=PARAMS,
        name="split_blocks",
    )(slots, source)


def sends_kernel(tables, blocks, low, high):
    gather_sends(tables, blocks, low, high)


def sends_of(tables, blocks):
    return pl.pallas_call(
        sends_kernel,
        in_specs=[SMEM, VMEM],
        out_specs=[VMEM] * 2,
        out_shape=[halo_blocks(), halo_blocks()],
        compiler_params=PARAMS,
        name="sends_of",
    )(tables, blocks)


def add_slots(total, batch):
    parts = [
        lax.dot_general(block, adj, (((1,), (1,)), ((), ())), preferred_element_type=F32)
        for block, adj, _ in batch
    ]
    for part, (_, _, row) in zip(parts, batch):
        total[row] = total[row] + part


def apply_own_kernel(tables, own, adj, total):
    total[...] = jnp.zeros_like(total)
    for start in range(0, adj.shape[0], BATCH):
        slots = range(start, start + BATCH)
        add_slots(total, [(own[tables[1, m]], adj[m], tables[2, m]) for m in slots])


def apply_own(tables, own, adj):
    return pl.pallas_call(
        apply_own_kernel,
        in_specs=[SMEM] + [VMEM] * 2,
        out_specs=VMEM,
        out_shape=jax.ShapeDtypeStruct((NBD + 1, FEATS, BLK), F32),
        compiler_params=PARAMS,
        name="apply_own",
    )(tables, own, adj)


def apply_halo_kernel(tables, begun, low, high, adj, out, total):
    total[...] = begun[...]
    for side, blocks in enumerate((low, high)):
        for start in range(0, HALO, BATCH):
            batch = []
            for k in range(start, start + BATCH):
                place = side * HALO + k
                batch.append((blocks[k], adj[tables[3, place]], tables[4, place]))
            add_slots(total, batch)
    out[...] = total[0:NBD].astype(BF16)


def apply_halo(tables, begun, low, high, adj):
    return pl.pallas_call(
        apply_halo_kernel,
        in_specs=[SMEM] + [VMEM] * 4,
        out_specs=VMEM,
        out_shape=blocks_of(),
        scratch_shapes=[pltpu.VMEM((NBD + 1, FEATS, BLK), F32)],
        compiler_params=PARAMS,
        name="apply_halo",
    )(tables, begun, low, high, adj)


def apply_blocks(tables, own, sends, adj):
    low, high = halo(*sends)
    return apply_halo(tables, apply_own(tables, own, adj), low, high, adj)


def rows_of(ref):
    parts = []
    for b in range(PER_GROUP):
        parts.append(
            jnp.concatenate([ref[g * PER_GROUP + b] for g in range(GROUPS)], axis=0)
        )
    return jnp.concatenate(parts, axis=1)


def put_rows(ref, values):
    for g in range(GROUPS):
        for b in range(PER_GROUP):
            ref[g * PER_GROUP + b] = values[
                g * FEATS : (g + 1) * FEATS, b * BLK : (b + 1) * BLK
            ]


def mix_one_kernel(spread, weight, hidden, slope):
    pre = lax.dot_general(
        weight[...], rows_of(spread), (((0,), (0,)), ((), ())), preferred_element_type=F32
    )
    sigma = sigmoid(pre)
    put_rows(hidden, (pre * sigma).astype(BF16))
    slope[...] = sigma * (1.0 + pre * (1.0 - sigma))


def mix_one(spread, weight):
    shape = (GROUPS * FEATS, PER_GROUP * BLK)
    return pl.pallas_call(
        mix_one_kernel,
        in_specs=[VMEM] * 2,
        out_specs=[VMEM] * 2,
        out_shape=[blocks_of(), jax.ShapeDtypeStruct(shape, F32)],
        compiler_params=PARAMS,
        name="mix_one",
    )(spread, weight)


def mix_two_kernel(spread, weight, pre_two):
    pre = lax.dot_general(
        weight[...], rows_of(spread), (((0,), (0,)), ((), ())), preferred_element_type=F32
    )
    put_rows(pre_two, pre.astype(BF16))


def mix_two(spread, weight):
    return pl.pallas_call(
        mix_two_kernel,
        in_specs=[VMEM] * 2,
        out_specs=VMEM,
        out_shape=blocks_of(),
        compiler_params=PARAMS,
        name="mix_two",
    )(spread, weight)


def turn_kernel(tables, pre_two, cotangent, delta, low, high):
    for b in range(NBD):
        pre = pre_two[b].astype(F32)
        sigma = sigmoid(pre)
        slope = sigma * (1.0 + pre * (1.0 - sigma))
        span = slice(b * BLK, (b + 1) * BLK)
        delta[b] = (cotangent[:, span].astype(F32) * slope).astype(BF16)
    gather_sends(tables, delta, low, high)


def turn(tables, pre_two, cotangent):
    return pl.pallas_call(
        turn_kernel,
        in_specs=[SMEM, VMEM, VMEM],
        out_specs=[VMEM] * 3,
        out_shape=[blocks_of(), halo_blocks(), halo_blocks()],
        compiler_params=PARAMS,
        name="turn",
    )(tables, pre_two, cotangent)


def apply_own_hidden_kernel(tables, own, adj, pre_two, total, hidden_out):
    apply_own_kernel(tables, own, adj, total)
    for b in range(NBD):
        pre = pre_two[b].astype(F32)
        hidden_out[:, b * BLK : (b + 1) * BLK] = (pre * sigmoid(pre)).astype(BF16)


def apply_own_hidden(tables, own, adj, pre_two):
    return pl.pallas_call(
        apply_own_hidden_kernel,
        in_specs=[SMEM] + [VMEM] * 3,
        out_specs=[VMEM] * 2,
        out_shape=[
            jax.ShapeDtypeStruct((NBD + 1, FEATS, BLK), F32),
            jax.ShapeDtypeStruct((FEATS, NBD * BLK), BF16),
        ],
        compiler_params=PARAMS,
        name="apply_own_hidden",
    )(tables, own, adj, pre_two)


def piece_places():
    for grad in range(2):
        for half in range(2):
            for part in range(GROUPS):
                place = (2 * grad + half) * GROUPS + part
                yield place, grad, slice(part * FEATS, (part + 1) * FEATS), slice(
                    half * BLK, (half + 1) * BLK
                )


def grads_kernel(back_two, spread_one, hidden_one, slope, weight, out):
    back = rows_of(back_two)
    along = (((1,), (1,)), ((), ()))
    carry = jnp.dot(weight[...], back, preferred_element_type=F32).astype(BF16)
    delta = (carry.astype(F32) * slope[...]).astype(BF16)
    sums = (
        lax.dot_general(rows_of(spread_one), delta, along, preferred_element_type=F32),
        lax.dot_general(rows_of(hidden_one), back, along, preferred_element_type=F32),
    )
    for place, grad, rows, columns in piece_places():
        out[place] = sums[grad][rows, columns].astype(BF16)


def grads(back_two, spread_one, hidden_one, slope, weight):
    return pl.pallas_call(
        grads_kernel,
        in_specs=[VMEM] * 5,
        out_specs=VMEM,
        out_shape=blocks_of(),
        compiler_params=PARAMS,
        name="grads",
    )(back_two, spread_one, hidden_one, slope, weight)


def finish_kernel(pieces, grad_one, grad_two):
    outs = (grad_one, grad_two)
    for place, grad, rows, columns in piece_places():
        outs[grad][rows, columns] = pieces[place].astype(F32)


def finish(pieces):
    size = GROUPS * FEATS
    return pl.pallas_call(
        finish_kernel,
        in_specs=[VMEM],
        out_specs=[VMEM] * 2,
        out_shape=[jax.ShapeDtypeStruct((size, size), F32)] * 2,
        compiler_params=PARAMS,
        name="finish",
    )(pieces)


def gather_pieces(piece, axes):
    spread = jnp.broadcast_to(piece[None], (lax.axis_size(axes),) + piece.shape)
    return exchange(spread, axes)


def sum_everywhere(partial):
    pieces = exchange(partial, PLANE).reshape(lax.axis_size(PLANE), -1, BLK)
    piece = jnp.sum(pieces.astype(F32), axis=0)
    piece = jnp.sum(gather_pieces(piece, "zlo"), axis=0).astype(BF16)
    piece = jnp.sum(gather_pieces(piece, "zhi").astype(F32), axis=0).astype(BF16)
    return gather_pieces(piece, PLANE).reshape(partial.shape)


def shards(
    features,
    weight_one,
    weight_two,
    blk_rows,
    blk_cols,
    blk_counts,
    adj_values,
    adj_tvalues,
    cotangent,
):
    base = lax.axis_index(NODE).astype(jnp.int32) * NBD
    spread = lambda scalar: jnp.broadcast_to(scalar, blk_rows.shape)
    slots = jnp.concatenate([blk_rows, blk_cols, spread(blk_counts[0]), spread(base)])
    tables, own, *sends = split_blocks(slots, features)
    spread_one = exchange(apply_blocks(tables, own, sends, adj_values), FEAT)
    hidden_rows, slope_one = mix_one(spread_one, weight_one)
    own = exchange(hidden_rows, FEAT)
    spread_two = exchange(apply_blocks(tables, own, sends_of(tables, own), adj_values), FEAT)
    pre_two = exchange(mix_two(spread_two, weight_two), FEAT)
    delta_two, *sends = turn(tables, pre_two, cotangent)
    low, high = halo(*sends)
    begun, hidden_out = apply_own_hidden(tables, delta_two, adj_tvalues, pre_two)
    back_two = exchange(apply_halo(tables, begun, low, high, adj_tvalues), FEAT)
    partial = grads(back_two, spread_one, hidden_rows, slope_one, weight_two)
    grad_one, grad_two = finish(sum_everywhere(partial))
    return (hidden_out, grad_one, grad_two)


def solution(mesh):
    fine = Mesh(np.asarray(mesh.devices).reshape(tuple(FINE.values())), tuple(FINE))
    return jax.shard_map(
        shards,
        mesh=fine,
        in_specs=(
            P(FEAT, NODE),
            P(),
            P(),
            P(NODE, None),
            P(NODE, None),
            P(NODE),
            P(NODE, None, None),
            P(NODE, None, None),
            P(FEAT, NODE),
        ),
        out_specs=(P(FEAT, NODE), P(), P()),
        check_vma=False,
    )
```

```python
import jax
import jax.numpy as jnp
import numpy as np
from jax import lax
from jax.experimental import pallas as pl
from jax.experimental.pallas import tpu as pltpu
from jax.sharding import Mesh, PartitionSpec as P

BLK = 128
NBD = 32
HALO = 16
GROUPS = 8
PER_GROUP = NBD // GROUPS
FEATS = 32
BATCH = 8
SIDE_KEY = 16384.0
BF16 = jnp.bfloat16
F32 = jnp.float32

FINE = {"x": 4, "zhi": 8, "zlo": 4, "y": 4, "core": 2}
NODE = ("x", "zhi", "zlo")
FEAT = ("y", "core")
PLANE = ("x", "y", "core")

SMEM = pl.BlockSpec(memory_space=pltpu.SMEM)
VMEM = pl.BlockSpec(memory_space=pltpu.VMEM)
PARAMS = pltpu.CompilerParams(vmem_limit_bytes=16 * 2**20)


def blocks_of(dtype=BF16):
    return jax.ShapeDtypeStruct((NBD, FEATS, BLK), dtype)


def halo_blocks():
    return jax.ShapeDtypeStruct((HALO, FEATS, BLK), BF16)


def exchange(array, axes):
    return lax.all_to_all(array, axes, split_axis=0, concat_axis=0, tiled=True)


def halo(send_low, send_high):
    count = lax.axis_size(NODE)
    forward = [(i, i + 1) for i in range(count - 1)]
    backward = [(target, source) for source, target in forward]
    low = lax.ppermute(send_high, NODE, forward)
    high = lax.ppermute(send_low, NODE, backward)
    return low, high


def turned(row):
    return jnp.transpose(jnp.broadcast_to(row, (BLK, row.shape[1])))


def rank(key, side):
    before = turned(key)
    earlier = (before < key) & (before >= side * SIDE_KEY)
    return jnp.sum(jnp.where(earlier, 1.0, 0.0), axis=0, keepdims=True)


def slot_tables(rows, cols, count, base):
    slot = lax.broadcasted_iota(jnp.int32, rows.shape, 1)
    live = slot < count
    local = (cols - base).astype(F32)
    rows = rows.astype(F32)
    low = live & (local < 0.0)
    high = live & (local >= float(NBD))
    side = jnp.where(low, 1.0, jnp.where(high, 2.0, 0.0))
    offset = side * SIDE_KEY
    shifted = local + float(NBD)
    send_rank = rank(offset + rows * BLK + shifted, side)
    recv_rank = rank(offset + shifted * BLK + rows, side)
    first = jnp.where(side > 0.0, (side - 1.0) * HALO, float(BLK))
    lane = lax.broadcasted_iota(jnp.int32, (BLK, BLK), 1).astype(F32)
    slots = lax.broadcasted_iota(jnp.int32, (BLK, BLK), 0).astype(F32)
    rows_down = turned(rows)
    sent = turned(first + send_rank) == lane
    received = turned(first + recv_rank) == lane
    total = lambda hit, values: jnp.sum(jnp.where(hit, values, 0.0), axis=0, keepdims=True)
    own = live & (side == 0.0)
    found = (
        total(sent, rows_down),
        jnp.where(own, local, 0.0),
        jnp.where(own, rows, float(NBD)),
        total(received, slots),
        NBD + total(received, rows_down - NBD),
    )
    return [table.astype(jnp.int32) for table in found]


def sigmoid(values):
    return 1.0 / (1.0 + jnp.exp(-values))


def gather_sends(tables, blocks, low, high):
    for k in range(HALO):
        low[k] = blocks[tables[0, k]]
        high[k] = blocks[tables[0, HALO + k]]


def split_kernel(slots, source, tables, blocks, low, high, scalar_tables, done):
    found = slot_tables(slots[0:1], slots[1:2], slots[2:3], slots[3:4])
    tables[...] = jnp.zeros_like(tables)
    for place, table in enumerate(found):
        tables[place : place + 1] = table
    copy = pltpu.make_async_copy(tables, scalar_tables, done)
    copy.start()
    for b in range(NBD):
        blocks[b] = source[:, b * BLK : (b + 1) * BLK]
    copy.wait()
    gather_sends(scalar_tables, blocks, low, high)


def split_blocks(slots, source):
    return pl.pallas_call(
        split_kernel,
        in_specs=[VMEM] * 2,
        out_specs=[VMEM] * 4,
        out_shape=[
            jax.ShapeDtypeStruct((8, BLK), jnp.int32),
            blocks_of(),
            halo_blocks(),
            halo_blocks(),
        ],
        scratch_shapes=[pltpu.SMEM((8, BLK), jnp.int32), pltpu.SemaphoreType.DMA],
        compiler_params=PARAMS,
        cost_estimate=pl.CostEstimate(flops=2**32, bytes_accessed=2**20, transcendentals=0),
        name="split_blocks",
    )(slots, source)


def sends_kernel(tables, blocks, low, high):
    gather_sends(tables, blocks, low, high)


def sends_of(tables, blocks):
    return pl.pallas_call(
        sends_kernel,
        in_specs=[SMEM, VMEM],
        out_specs=[VMEM] * 2,
        out_shape=[halo_blocks(), halo_blocks()],
        compiler_params=PARAMS,
        name="sends_of",
    )(tables, blocks)


def add_slots(total, batch):
    parts = [
        lax.dot_general(block, adj, (((1,), (1,)), ((), ())), preferred_element_type=F32)
        for block, adj, _ in batch
    ]
    for part, (_, _, row) in zip(parts, batch):
        total[row] = total[row] + part


def apply_own_kernel(tables, own, adj, total):
    total[...] = jnp.zeros_like(total)
    for start in range(0, adj.shape[0], BATCH):
        slots = range(start, start + BATCH)
        add_slots(total, [(own[tables[1, m]], adj[m], tables[2, m]) for m in slots])


def apply_own(tables, own, adj):
    return pl.pallas_call(
        apply_own_kernel,
        in_specs=[SMEM] + [VMEM] * 2,
        out_specs=VMEM,
        out_shape=jax.ShapeDtypeStruct((NBD + 1, FEATS, BLK), F32),
        compiler_params=PARAMS,
        name="apply_own",
    )(tables, own, adj)


def apply_halo_kernel(tables, begun, low, high, adj, out, total):
    total[...] = begun[...]
    for side, blocks in enumerate((low, high)):
        for start in range(0, HALO, BATCH):
            batch = []
            for k in range(start, start + BATCH):
                place = side * HALO + k
                batch.append((blocks[k], adj[tables[3, place]], tables[4, place]))
            add_slots(total, batch)
    out[...] = total[0:NBD].astype(BF16)


def apply_halo(tables, begun, low, high, adj):
    return pl.pallas_call(
        apply_halo_kernel,
        in_specs=[SMEM] + [VMEM] * 4,
        out_specs=VMEM,
        out_shape=blocks_of(),
        scratch_shapes=[pltpu.VMEM((NBD + 1, FEATS, BLK), F32)],
        compiler_params=PARAMS,
        name="apply_halo",
    )(tables, begun, low, high, adj)


def apply_blocks(tables, own, sends, adj):
    low, high = halo(*sends)
    return apply_halo(tables, apply_own(tables, own, adj), low, high, adj)


def rows_of(ref):
    parts = []
    for b in range(PER_GROUP):
        parts.append(
            jnp.concatenate([ref[g * PER_GROUP + b] for g in range(GROUPS)], axis=0)
        )
    return jnp.concatenate(parts, axis=1)


def put_rows(ref, values):
    for g in range(GROUPS):
        for b in range(PER_GROUP):
            ref[g * PER_GROUP + b] = values[
                g * FEATS : (g + 1) * FEATS, b * BLK : (b + 1) * BLK
            ]


def mix_one_kernel(spread, weight, hidden, slope):
    pre = lax.dot_general(
        weight[...], rows_of(spread), (((0,), (0,)), ((), ())), preferred_element_type=F32
    )
    sigma = sigmoid(pre)
    put_rows(hidden, (pre * sigma).astype(BF16))
    slope[...] = sigma * (1.0 + pre * (1.0 - sigma))


def mix_one(spread, weight):
    shape = (GROUPS * FEATS, PER_GROUP * BLK)
    return pl.pallas_call(
        mix_one_kernel,
        in_specs=[VMEM] * 2,
        out_specs=[VMEM] * 2,
        out_shape=[blocks_of(), jax.ShapeDtypeStruct(shape, F32)],
        compiler_params=PARAMS,
        name="mix_one",
    )(spread, weight)


def mix_two_kernel(spread, weight, pre_two):
    pre = lax.dot_general(
        weight[...], rows_of(spread), (((0,), (0,)), ((), ())), preferred_element_type=F32
    )
    put_rows(pre_two, pre.astype(BF16))


def mix_two(spread, weight):
    return pl.pallas_call(
        mix_two_kernel,
        in_specs=[VMEM] * 2,
        out_specs=VMEM,
        out_shape=blocks_of(),
        compiler_params=PARAMS,
        name="mix_two",
    )(spread, weight)


def turn_kernel(tables, pre_two, cotangent, delta, low, high):
    for b in range(NBD):
        pre = pre_two[b].astype(F32)
        sigma = sigmoid(pre)
        slope = sigma * (1.0 + pre * (1.0 - sigma))
        span = slice(b * BLK, (b + 1) * BLK)
        delta[b] = (cotangent[:, span].astype(F32) * slope).astype(BF16)
    gather_sends(tables, delta, low, high)


def turn(tables, pre_two, cotangent):
    return pl.pallas_call(
        turn_kernel,
        in_specs=[SMEM, VMEM, VMEM],
        out_specs=[VMEM] * 3,
        out_shape=[blocks_of(), halo_blocks(), halo_blocks()],
        compiler_params=PARAMS,
        name="turn",
    )(tables, pre_two, cotangent)


def apply_own_hidden_kernel(tables, own, adj, pre_two, total, hidden_out):
    apply_own_kernel(tables, own, adj, total)
    for b in range(NBD):
        pre = pre_two[b].astype(F32)
        hidden_out[:, b * BLK : (b + 1) * BLK] = (pre * sigmoid(pre)).astype(BF16)


def apply_own_hidden(tables, own, adj, pre_two):
    return pl.pallas_call(
        apply_own_hidden_kernel,
        in_specs=[SMEM] + [VMEM] * 3,
        out_specs=[VMEM] * 2,
        out_shape=[
            jax.ShapeDtypeStruct((NBD + 1, FEATS, BLK), F32),
            jax.ShapeDtypeStruct((FEATS, NBD * BLK), BF16),
        ],
        compiler_params=PARAMS,
        name="apply_own_hidden",
    )(tables, own, adj, pre_two)


def piece_places():
    for grad in range(2):
        for half in range(2):
            for part in range(GROUPS):
                place = (2 * grad + half) * GROUPS + part
                yield place, grad, slice(part * FEATS, (part + 1) * FEATS), slice(
                    half * BLK, (half + 1) * BLK
                )


def grads_kernel(back_two, spread_one, hidden_one, slope, weight, out):
    back = rows_of(back_two)
    along = (((1,), (1,)), ((), ()))
    carry = jnp.dot(weight[...], back, preferred_element_type=F32).astype(BF16)
    delta = (carry.astype(F32) * slope[...]).astype(BF16)
    sums = (
        lax.dot_general(rows_of(spread_one), delta, along, preferred_element_type=F32),
        lax.dot_general(rows_of(hidden_one), back, along, preferred_element_type=F32),
    )
    for place, grad, rows, columns in piece_places():
        out[place] = sums[grad][rows, columns].astype(BF16)


def grads(back_two, spread_one, hidden_one, slope, weight):
    return pl.pallas_call(
        grads_kernel,
        in_specs=[VMEM] * 5,
        out_specs=VMEM,
        out_shape=blocks_of(),
        compiler_params=PARAMS,
        name="grads",
    )(back_two, spread_one, hidden_one, slope, weight)


def finish_kernel(pieces, grad_one, grad_two):
    outs = (grad_one, grad_two)
    for place, grad, rows, columns in piece_places():
        outs[grad][rows, columns] = pieces[place].astype(F32)


def finish(pieces):
    size = GROUPS * FEATS
    return pl.pallas_call(
        finish_kernel,
        in_specs=[VMEM],
        out_specs=[VMEM] * 2,
        out_shape=[jax.ShapeDtypeStruct((size, size), F32)] * 2,
        compiler_params=PARAMS,
        name="finish",
    )(pieces)


def gather_pieces(piece, axes):
    spread = jnp.broadcast_to(piece[None], (lax.axis_size(axes),) + piece.shape)
    return exchange(spread, axes)


def sum_everywhere(partial):
    pieces = exchange(partial, PLANE).reshape(lax.axis_size(PLANE), -1, BLK)
    piece = jnp.sum(pieces.astype(F32), axis=0).astype(BF16)
    piece = jnp.sum(gather_pieces(piece, "zlo").astype(F32), axis=0).astype(BF16)
    piece = jnp.sum(gather_pieces(piece, "zhi").astype(F32), axis=0).astype(BF16)
    return gather_pieces(piece, PLANE).reshape(partial.shape)


def shards(
    features,
    weight_one,
    weight_two,
    blk_rows,
    blk_cols,
    blk_counts,
    adj_values,
    adj_tvalues,
    cotangent,
):
    base = lax.axis_index(NODE).astype(jnp.int32) * NBD
    spread = lambda scalar: jnp.broadcast_to(scalar, blk_rows.shape)
    slots = jnp.concatenate([blk_rows, blk_cols, spread(blk_counts[0]), spread(base)])
    tables, own, *sends = split_blocks(slots, features)
    spread_one = exchange(apply_blocks(tables, own, sends, adj_values), FEAT)
    hidden_rows, slope_one = mix_one(spread_one, weight_one)
    own = exchange(hidden_rows, FEAT)
    spread_two = exchange(apply_blocks(tables, own, sends_of(tables, own), adj_values), FEAT)
    pre_two = exchange(mix_two(spread_two, weight_two), FEAT)
    delta_two, *sends = turn(tables, pre_two, cotangent)
    low, high = halo(*sends)
    begun, hidden_out = apply_own_hidden(tables, delta_two, adj_tvalues, pre_two)
    back_two = exchange(apply_halo(tables, begun, low, high, adj_tvalues), FEAT)
    partial = grads(back_two, spread_one, hidden_rows, slope_one, weight_two)
    grad_one, grad_two = finish(sum_everywhere(partial))
    return (hidden_out, grad_one, grad_two)


def solution(mesh):
    fine = Mesh(np.asarray(mesh.devices).reshape(tuple(FINE.values())), tuple(FINE))
    return jax.shard_map(
        shards,
        mesh=fine,
        in_specs=(
            P(FEAT, NODE),
            P(),
            P(),
            P(NODE, None),
            P(NODE, None),
            P(NODE),
            P(NODE, None, None),
            P(NODE, None, None),
            P(FEAT, NODE),
        ),
        out_specs=(P(FEAT, NODE), P(), P()),
        check_vma=False,
    )
```

```python
import jax
import jax.numpy as jnp
import numpy as np
from jax import lax
from jax.experimental import pallas as pl
from jax.experimental.pallas import tpu as pltpu
from jax.sharding import Mesh, PartitionSpec as P

BLK = 128
NBD = 32
HALO = 16
GROUPS = 8
PER_GROUP = NBD // GROUPS
FEATS = 32
BATCH = 8
SIDE_KEY = 16384.0
BF16 = jnp.bfloat16
F32 = jnp.float32

FINE = {"x": 4, "zhi": 8, "zlo": 4, "y": 4, "core": 2}
NODE = ("x", "zhi", "zlo")
FEAT = ("y", "core")
PLANE = ("x", "y", "core")

SMEM = pl.BlockSpec(memory_space=pltpu.SMEM)
VMEM = pl.BlockSpec(memory_space=pltpu.VMEM)
PARAMS = pltpu.CompilerParams(vmem_limit_bytes=16 * 2**20)


def blocks_of(dtype=BF16):
    return jax.ShapeDtypeStruct((NBD, FEATS, BLK), dtype)


def halo_blocks():
    return jax.ShapeDtypeStruct((HALO, FEATS, BLK), BF16)


def exchange(array, axes):
    return lax.all_to_all(array, axes, split_axis=0, concat_axis=0, tiled=True)


def halo(send_low, send_high):
    count = lax.axis_size(NODE)
    forward = [(i, i + 1) for i in range(count - 1)]
    backward = [(target, source) for source, target in forward]
    low = lax.ppermute(send_high, NODE, forward)
    high = lax.ppermute(send_low, NODE, backward)
    return low, high


def turned(row):
    return jnp.transpose(jnp.broadcast_to(row, (BLK, row.shape[1])))


def rank(key, side):
    before = turned(key)
    earlier = (before < key) & (before >= side * SIDE_KEY)
    return jnp.sum(jnp.where(earlier, 1.0, 0.0), axis=0, keepdims=True)


def slot_tables(rows, cols, count, base):
    slot = lax.broadcasted_iota(jnp.int32, rows.shape, 1)
    live = slot < count
    local = (cols - base).astype(F32)
    rows = rows.astype(F32)
    low = live & (local < 0.0)
    high = live & (local >= float(NBD))
    side = jnp.where(low, 1.0, jnp.where(high, 2.0, 0.0))
    offset = side * SIDE_KEY
    shifted = local + float(NBD)
    send_rank = rank(offset + rows * BLK + shifted, side)
    recv_rank = rank(offset + shifted * BLK + rows, side)
    first = jnp.where(side > 0.0, (side - 1.0) * HALO, float(BLK))
    lane = lax.broadcasted_iota(jnp.int32, (BLK, BLK), 1).astype(F32)
    slots = lax.broadcasted_iota(jnp.int32, (BLK, BLK), 0).astype(F32)
    rows_down = turned(rows)
    sent = turned(first + send_rank) == lane
    received = turned(first + recv_rank) == lane
    total = lambda hit, values: jnp.sum(jnp.where(hit, values, 0.0), axis=0, keepdims=True)
    own = live & (side == 0.0)
    found = (
        total(sent, rows_down),
        jnp.where(own, local, 0.0),
        jnp.where(own, rows, float(NBD)),
        total(received, slots),
        NBD + total(received, rows_down - NBD),
        jnp.where(own, rows, 0.0),
        jnp.where(own, local, float(NBD)),
    )
    return [table.astype(jnp.int32) for table in found]


def sigmoid(values):
    return 1.0 / (1.0 + jnp.exp(-values))


def gather_sends(tables, blocks, low, high):
    for k in range(HALO):
        low[k] = blocks[tables[0, k]]
        high[k] = blocks[tables[0, HALO + k]]


def split_kernel(slots, source, tables, blocks, low, high, scalar_tables, done):
    found = slot_tables(slots[0:1], slots[1:2], slots[2:3], slots[3:4])
    tables[...] = jnp.zeros_like(tables)
    for place, table in enumerate(found):
        tables[place : place + 1] = table
    copy = pltpu.make_async_copy(tables, scalar_tables, done)
    copy.start()
    for b in range(NBD):
        blocks[b] = source[:, b * BLK : (b + 1) * BLK]
    copy.wait()
    gather_sends(scalar_tables, blocks, low, high)


def split_blocks(slots, source):
    return pl.pallas_call(
        split_kernel,
        in_specs=[VMEM] * 2,
        out_specs=[VMEM] * 4,
        out_shape=[
            jax.ShapeDtypeStruct((8, BLK), jnp.int32),
            blocks_of(),
            halo_blocks(),
            halo_blocks(),
        ],
        scratch_shapes=[pltpu.SMEM((8, BLK), jnp.int32), pltpu.SemaphoreType.DMA],
        compiler_params=PARAMS,
        cost_estimate=pl.CostEstimate(flops=2**32, bytes_accessed=2**20, transcendentals=0),
        name="split_blocks",
    )(slots, source)


def sends_kernel(tables, blocks, low, high):
    gather_sends(tables, blocks, low, high)


def sends_of(tables, blocks):
    return pl.pallas_call(
        sends_kernel,
        in_specs=[SMEM, VMEM],
        out_specs=[VMEM] * 2,
        out_shape=[halo_blocks(), halo_blocks()],
        compiler_params=PARAMS,
        name="sends_of",
    )(tables, blocks)


def add_slots(total, batch, adj_axis=1):
    along = (((1,), (adj_axis,)), ((), ()))
    parts = [
        lax.dot_general(block, adj, along, preferred_element_type=F32)
        for block, adj, _ in batch
    ]
    for part, (_, _, row) in zip(parts, batch):
        total[row] = total[row] + part


def apply_own_kernel(tables, own, adj, total):
    total[...] = jnp.zeros_like(total)
    for start in range(0, adj.shape[0], BATCH):
        slots = range(start, start + BATCH)
        add_slots(total, [(own[tables[1, m]], adj[m], tables[2, m]) for m in slots])


def apply_own(tables, own, adj):
    return pl.pallas_call(
        apply_own_kernel,
        in_specs=[SMEM] + [VMEM] * 2,
        out_specs=VMEM,
        out_shape=jax.ShapeDtypeStruct((NBD + 1, FEATS, BLK), F32),
        compiler_params=PARAMS,
        name="apply_own",
    )(tables, own, adj)


def apply_halo_kernel(tables, begun, low, high, adj, out, total):
    total[...] = begun[...]
    for side, blocks in enumerate((low, high)):
        for start in range(0, HALO, BATCH):
            batch = []
            for k in range(start, start + BATCH):
                place = side * HALO + k
                batch.append((blocks[k], adj[tables[3, place]], tables[4, place]))
            add_slots(total, batch)
    out[...] = total[0:NBD].astype(BF16)


def apply_halo(tables, begun, low, high, adj):
    return pl.pallas_call(
        apply_halo_kernel,
        in_specs=[SMEM] + [VMEM] * 4,
        out_specs=VMEM,
        out_shape=blocks_of(),
        scratch_shapes=[pltpu.VMEM((NBD + 1, FEATS, BLK), F32)],
        compiler_params=PARAMS,
        name="apply_halo",
    )(tables, begun, low, high, adj)


def apply_blocks(tables, own, sends, adj):
    low, high = halo(*sends)
    return apply_halo(tables, apply_own(tables, own, adj), low, high, adj)


def rows_of(ref):
    parts = []
    for b in range(PER_GROUP):
        parts.append(
            jnp.concatenate([ref[g * PER_GROUP + b] for g in range(GROUPS)], axis=0)
        )
    return jnp.concatenate(parts, axis=1)


def put_rows(ref, values):
    for g in range(GROUPS):
        for b in range(PER_GROUP):
            ref[g * PER_GROUP + b] = values[
                g * FEATS : (g + 1) * FEATS, b * BLK : (b + 1) * BLK
            ]


def mix_one_kernel(spread, weight, hidden, slope):
    pre = lax.dot_general(
        weight[...], rows_of(spread), (((0,), (0,)), ((), ())), preferred_element_type=F32
    )
    sigma = sigmoid(pre)
    put_rows(hidden, (pre * sigma).astype(BF16))
    slope[...] = sigma * (1.0 + pre * (1.0 - sigma))


def mix_one(spread, weight):
    shape = (GROUPS * FEATS, PER_GROUP * BLK)
    return pl.pallas_call(
        mix_one_kernel,
        in_specs=[VMEM] * 2,
        out_specs=[VMEM] * 2,
        out_shape=[blocks_of(), jax.ShapeDtypeStruct(shape, F32)],
        compiler_params=PARAMS,
        name="mix_one",
    )(spread, weight)


def mix_two_kernel(spread, weight, pre_two):
    pre = lax.dot_general(
        weight[...], rows_of(spread), (((0,), (0,)), ((), ())), preferred_element_type=F32
    )
    put_rows(pre_two, pre.astype(BF16))


def mix_two(spread, weight):
    return pl.pallas_call(
        mix_two_kernel,
        in_specs=[VMEM] * 2,
        out_specs=VMEM,
        out_shape=blocks_of(),
        compiler_params=PARAMS,
        name="mix_two",
    )(spread, weight)


def turn_kernel(tables, pre_two, cotangent, delta, low, high):
    for b in range(NBD):
        pre = pre_two[b].astype(F32)
        sigma = sigmoid(pre)
        slope = sigma * (1.0 + pre * (1.0 - sigma))
        span = slice(b * BLK, (b + 1) * BLK)
        delta[b] = (cotangent[:, span].astype(F32) * slope).astype(BF16)
    gather_sends(tables, delta, low, high)


def turn(tables, pre_two, cotangent):
    return pl.pallas_call(
        turn_kernel,
        in_specs=[SMEM, VMEM, VMEM],
        out_specs=[VMEM] * 3,
        out_shape=[blocks_of(), halo_blocks(), halo_blocks()],
        compiler_params=PARAMS,
        name="turn",
    )(tables, pre_two, cotangent)


def push_own_hidden_kernel(tables, own, adj, pre_two, total, hidden_out):
    total[...] = jnp.zeros_like(total)
    for start in range(0, adj.shape[0], BATCH):
        slots = range(start, start + BATCH)
        add_slots(total, [(own[tables[5, m]], adj[m], tables[6, m]) for m in slots], 0)
    for b in range(NBD):
        pre = pre_two[b].astype(F32)
        hidden_out[:, b * BLK : (b + 1) * BLK] = (pre * sigmoid(pre)).astype(BF16)


def push_own_hidden(tables, own, adj, pre_two):
    return pl.pallas_call(
        push_own_hidden_kernel,
        in_specs=[SMEM] + [VMEM] * 3,
        out_specs=[VMEM] * 2,
        out_shape=[
            jax.ShapeDtypeStruct((NBD + 1, FEATS, BLK), F32),
            jax.ShapeDtypeStruct((FEATS, NBD * BLK), BF16),
        ],
        compiler_params=PARAMS,
        name="push_own_hidden",
    )(tables, own, adj, pre_two)


def piece_places():
    for grad in range(2):
        for half in range(2):
            for part in range(GROUPS):
                place = (2 * grad + half) * GROUPS + part
                yield place, grad, slice(part * FEATS, (part + 1) * FEATS), slice(
                    half * BLK, (half + 1) * BLK
                )


def grads_kernel(back_two, spread_one, hidden_one, slope, weight, out):
    back = rows_of(back_two)
    along = (((1,), (1,)), ((), ()))
    carry = jnp.dot(weight[...], back, preferred_element_type=F32).astype(BF16)
    delta = (carry.astype(F32) * slope[...]).astype(BF16)
    sums = (
        lax.dot_general(rows_of(spread_one), delta, along, preferred_element_type=F32),
        lax.dot_general(rows_of(hidden_one), back, along, preferred_element_type=F32),
    )
    for place, grad, rows, columns in piece_places():
        out[place] = sums[grad][rows, columns].astype(BF16)


def grads(back_two, spread_one, hidden_one, slope, weight):
    return pl.pallas_call(
        grads_kernel,
        in_specs=[VMEM] * 5,
        out_specs=VMEM,
        out_shape=blocks_of(),
        compiler_params=PARAMS,
        name="grads",
    )(back_two, spread_one, hidden_one, slope, weight)


def finish_kernel(pieces, grad_one, grad_two):
    outs = (grad_one, grad_two)
    for place, grad, rows, columns in piece_places():
        outs[grad][rows, columns] = pieces[place].astype(F32)


def finish(pieces):
    size = GROUPS * FEATS
    return pl.pallas_call(
        finish_kernel,
        in_specs=[VMEM],
        out_specs=[VMEM] * 2,
        out_shape=[jax.ShapeDtypeStruct((size, size), F32)] * 2,
        compiler_params=PARAMS,
        name="finish",
    )(pieces)


def gather_pieces(piece, axes):
    spread = jnp.broadcast_to(piece[None], (lax.axis_size(axes),) + piece.shape)
    return exchange(spread, axes)


def sum_everywhere(partial):
    pieces = exchange(partial, PLANE).reshape(lax.axis_size(PLANE), -1, BLK)
    piece = jnp.sum(pieces.astype(F32), axis=0).astype(BF16)
    piece = jnp.sum(gather_pieces(piece, "zlo").astype(F32), axis=0).astype(BF16)
    piece = jnp.sum(gather_pieces(piece, "zhi").astype(F32), axis=0).astype(BF16)
    return gather_pieces(piece, PLANE).reshape(partial.shape)


def shards(
    features,
    weight_one,
    weight_two,
    blk_rows,
    blk_cols,
    blk_counts,
    adj_values,
    adj_tvalues,
    cotangent,
):
    base = lax.axis_index(NODE).astype(jnp.int32) * NBD
    spread = lambda scalar: jnp.broadcast_to(scalar, blk_rows.shape)
    slots = jnp.concatenate([blk_rows, blk_cols, spread(blk_counts[0]), spread(base)])
    tables, own, *sends = split_blocks(slots, features)
    spread_one = exchange(apply_blocks(tables, own, sends, adj_values), FEAT)
    hidden_rows, slope_one = mix_one(spread_one, weight_one)
    own = exchange(hidden_rows, FEAT)
    spread_two = exchange(apply_blocks(tables, own, sends_of(tables, own), adj_values), FEAT)
    pre_two = exchange(mix_two(spread_two, weight_two), FEAT)
    delta_two, *sends = turn(tables, pre_two, cotangent)
    low, high = halo(*sends)
    begun, hidden_out = push_own_hidden(tables, delta_two, adj_values, pre_two)
    back_two = exchange(apply_halo(tables, begun, low, high, adj_tvalues), FEAT)
    partial = grads(back_two, spread_one, hidden_rows, slope_one, weight_two)
    grad_one, grad_two = finish(sum_everywhere(partial))
    return (hidden_out, grad_one, grad_two)


def solution(mesh):
    fine = Mesh(np.asarray(mesh.devices).reshape(tuple(FINE.values())), tuple(FINE))
    return jax.shard_map(
        shards,
        mesh=fine,
        in_specs=(
            P(FEAT, NODE),
            P(),
            P(),
            P(NODE, None),
            P(NODE, None),
            P(NODE),
            P(NODE, None, None),
            P(NODE, None, None),
            P(FEAT, NODE),
        ),
        out_specs=(P(FEAT, NODE), P(), P()),
        check_vma=False,
    )
```

```python
import jax
import jax.numpy as jnp
import numpy as np
from jax import lax
from jax.experimental import pallas as pl
from jax.experimental.pallas import tpu as pltpu
from jax.sharding import Mesh, PartitionSpec as P

BLK = 128
NBD = 32
HALO = 16
GROUPS = 8
PER_GROUP = NBD // GROUPS
FEATS = 32
BATCH = 8
SIDE_KEY = 16384.0
BF16 = jnp.bfloat16
F32 = jnp.float32

FINE = {"x": 4, "zhi": 8, "zlo": 4, "y": 4, "core": 2}
NODE = ("x", "zhi", "zlo")
FEAT = ("y", "core")
PLANE = ("x", "y", "core")

SMEM = pl.BlockSpec(memory_space=pltpu.SMEM)
VMEM = pl.BlockSpec(memory_space=pltpu.VMEM)
PARAMS = pltpu.CompilerParams(vmem_limit_bytes=16 * 2**20)


def blocks_of(dtype=BF16):
    return jax.ShapeDtypeStruct((NBD, FEATS, BLK), dtype)


def halo_blocks():
    return jax.ShapeDtypeStruct((HALO, FEATS, BLK), BF16)


def exchange(array, axes):
    return lax.all_to_all(array, axes, split_axis=0, concat_axis=0, tiled=True)


def halo(send_low, send_high):
    count = lax.axis_size(NODE)
    forward = [(i, i + 1) for i in range(count - 1)]
    backward = [(target, source) for source, target in forward]
    low = lax.ppermute(send_high, NODE, forward)
    high = lax.ppermute(send_low, NODE, backward)
    return low, high


def turned(row):
    return jnp.transpose(jnp.broadcast_to(row, (BLK, row.shape[1])))


def rank(key, side):
    before = turned(key)
    earlier = (before < key) & (before >= side * SIDE_KEY)
    return jnp.sum(jnp.where(earlier, 1.0, 0.0), axis=0, keepdims=True)


def slot_tables(rows, cols, count, base):
    slot = lax.broadcasted_iota(jnp.int32, rows.shape, 1)
    live = slot < count
    local = (cols - base).astype(F32)
    rows = rows.astype(F32)
    low = live & (local < 0.0)
    high = live & (local >= float(NBD))
    side = jnp.where(low, 1.0, jnp.where(high, 2.0, 0.0))
    offset = side * SIDE_KEY
    shifted = local + float(NBD)
    send_rank = rank(offset + rows * BLK + shifted, side)
    recv_rank = rank(offset + shifted * BLK + rows, side)
    first = jnp.where(side > 0.0, (side - 1.0) * HALO, float(BLK))
    lane = lax.broadcasted_iota(jnp.int32, (BLK, BLK), 1).astype(F32)
    slots = lax.broadcasted_iota(jnp.int32, (BLK, BLK), 0).astype(F32)
    rows_down = turned(rows)
    sent = turned(first + send_rank) == lane
    received = turned(first + recv_rank) == lane
    total = lambda hit, values: jnp.sum(jnp.where(hit, values, 0.0), axis=0, keepdims=True)
    own = live & (side == 0.0)
    found = (
        total(sent, rows_down),
        jnp.where(own, local, 0.0),
        jnp.where(own, rows, float(NBD)),
        total(received, slots),
        NBD + total(received, rows_down - NBD),
        jnp.where(own, rows, 0.0),
        jnp.where(own, local, float(NBD)),
    )
    return [table.astype(jnp.int32) for table in found]


def sigmoid(values):
    return 1.0 / (1.0 + jnp.exp(-values))


def gather_sends(tables, blocks, low, high):
    for k in range(HALO):
        low[k] = blocks[tables[0, k]]
        high[k] = blocks[tables[0, HALO + k]]


def split_kernel(slots, source, tables, blocks, low, high, scalar_tables, done):
    found = slot_tables(slots[0:1], slots[1:2], slots[2:3], slots[3:4])
    tables[...] = jnp.zeros_like(tables)
    for place, table in enumerate(found):
        tables[place : place + 1] = table
    copy = pltpu.make_async_copy(tables, scalar_tables, done)
    copy.start()
    for b in range(NBD):
        blocks[b] = source[:, b * BLK : (b + 1) * BLK]
    copy.wait()
    gather_sends(scalar_tables, blocks, low, high)


def split_blocks(slots, source):
    return pl.pallas_call(
        split_kernel,
        in_specs=[VMEM] * 2,
        out_specs=[VMEM] * 4,
        out_shape=[
            jax.ShapeDtypeStruct((8, BLK), jnp.int32),
            blocks_of(),
            halo_blocks(),
            halo_blocks(),
        ],
        scratch_shapes=[pltpu.SMEM((8, BLK), jnp.int32), pltpu.SemaphoreType.DMA],
        compiler_params=PARAMS,
        cost_estimate=pl.CostEstimate(flops=2**32, bytes_accessed=2**20, transcendentals=0),
        name="split_blocks",
    )(slots, source)


def sends_kernel(tables, blocks, low, high):
    gather_sends(tables, blocks, low, high)


def sends_of(tables, blocks):
    return pl.pallas_call(
        sends_kernel,
        in_specs=[SMEM, VMEM],
        out_specs=[VMEM] * 2,
        out_shape=[halo_blocks(), halo_blocks()],
        compiler_params=PARAMS,
        name="sends_of",
    )(tables, blocks)


def add_slots(total, batch, adj_axis=1):
    along = (((1,), (adj_axis,)), ((), ()))
    parts = [
        lax.dot_general(block, adj, along, preferred_element_type=F32)
        for block, adj, _ in batch
    ]
    for part, (_, _, row) in zip(parts, batch):
        total[row] = total[row] + part


def apply_own_kernel(tables, own, adj, total):
    total[...] = jnp.zeros_like(total)
    for start in range(0, adj.shape[0], BATCH):
        slots = range(start, start + BATCH)
        add_slots(total, [(own[tables[1, m]], adj[m], tables[2, m]) for m in slots])


def apply_own(tables, own, adj):
    return pl.pallas_call(
        apply_own_kernel,
        in_specs=[SMEM] + [VMEM] * 2,
        out_specs=VMEM,
        out_shape=jax.ShapeDtypeStruct((NBD + 1, FEATS, BLK), F32),
        compiler_params=PARAMS,
        name="apply_own",
    )(tables, own, adj)


def add_side(tables, total, blocks, adj, side):
    for start in range(0, HALO, BATCH):
        batch = []
        for k in range(start, start + BATCH):
            place = side * HALO + k
            batch.append((blocks[k], adj[tables[3, place]], tables[4, place]))
        add_slots(total, batch)


def apply_low_kernel(tables, begun, low, adj, total):
    total[...] = begun[...]
    add_side(tables, total, low, adj, 0)


def apply_high_kernel(tables, begun, high, adj, out, total):
    total[...] = begun[...]
    add_side(tables, total, high, adj, 1)
    out[...] = total[0:NBD].astype(BF16)


def apply_halo(tables, begun, low, high, adj):
    totals = (NBD + 1, FEATS, BLK)
    begun = pl.pallas_call(
        apply_low_kernel,
        in_specs=[SMEM] + [VMEM] * 3,
        out_specs=VMEM,
        out_shape=jax.ShapeDtypeStruct(totals, F32),
        compiler_params=PARAMS,
        name="apply_low",
    )(tables, begun, low, adj)
    return pl.pallas_call(
        apply_high_kernel,
        in_specs=[SMEM] + [VMEM] * 3,
        out_specs=VMEM,
        out_shape=blocks_of(),
        scratch_shapes=[pltpu.VMEM(totals, F32)],
        compiler_params=PARAMS,
        name="apply_high",
    )(tables, begun, high, adj)


def apply_blocks(tables, own, sends, adj):
    low, high = halo(*sends)
    return apply_halo(tables, apply_own(tables, own, adj), low, high, adj)


def rows_of(ref):
    parts = []
    for b in range(PER_GROUP):
        parts.append(
            jnp.concatenate([ref[g * PER_GROUP + b] for g in range(GROUPS)], axis=0)
        )
    return jnp.concatenate(parts, axis=1)


def put_rows(ref, values):
    for g in range(GROUPS):
        for b in range(PER_GROUP):
            ref[g * PER_GROUP + b] = values[
                g * FEATS : (g + 1) * FEATS, b * BLK : (b + 1) * BLK
            ]


def mix_one_kernel(spread, weight, hidden, slope):
    pre = lax.dot_general(
        weight[...], rows_of(spread), (((0,), (0,)), ((), ())), preferred_element_type=F32
    )
    sigma = sigmoid(pre)
    put_rows(hidden, (pre * sigma).astype(BF16))
    slope[...] = sigma * (1.0 + pre * (1.0 - sigma))


def mix_one(spread, weight):
    shape = (GROUPS * FEATS, PER_GROUP * BLK)
    return pl.pallas_call(
        mix_one_kernel,
        in_specs=[VMEM] * 2,
        out_specs=[VMEM] * 2,
        out_shape=[blocks_of(), jax.ShapeDtypeStruct(shape, F32)],
        compiler_params=PARAMS,
        name="mix_one",
    )(spread, weight)


def mix_two_kernel(spread, weight, pre_two):
    pre = lax.dot_general(
        weight[...], rows_of(spread), (((0,), (0,)), ((), ())), preferred_element_type=F32
    )
    put_rows(pre_two, pre.astype(BF16))


def mix_two(spread, weight):
    return pl.pallas_call(
        mix_two_kernel,
        in_specs=[VMEM] * 2,
        out_specs=VMEM,
        out_shape=blocks_of(),
        compiler_params=PARAMS,
        name="mix_two",
    )(spread, weight)


def turn_kernel(tables, pre_two, cotangent, delta, low, high):
    for b in range(NBD):
        pre = pre_two[b].astype(F32)
        sigma = sigmoid(pre)
        slope = sigma * (1.0 + pre * (1.0 - sigma))
        span = slice(b * BLK, (b + 1) * BLK)
        delta[b] = (cotangent[:, span].astype(F32) * slope).astype(BF16)
    gather_sends(tables, delta, low, high)


def turn(tables, pre_two, cotangent):
    return pl.pallas_call(
        turn_kernel,
        in_specs=[SMEM, VMEM, VMEM],
        out_specs=[VMEM] * 3,
        out_shape=[blocks_of(), halo_blocks(), halo_blocks()],
        compiler_params=PARAMS,
        name="turn",
    )(tables, pre_two, cotangent)


def push_own_hidden_kernel(tables, own, adj, pre_two, total, hidden_out):
    total[...] = jnp.zeros_like(total)
    for start in range(0, adj.shape[0], BATCH):
        slots = range(start, start + BATCH)
        add_slots(total, [(own[tables[5, m]], adj[m], tables[6, m]) for m in slots], 0)
    for b in range(NBD):
        pre = pre_two[b].astype(F32)
        hidden_out[:, b * BLK : (b + 1) * BLK] = (pre * sigmoid(pre)).astype(BF16)


def push_own_hidden(tables, own, adj, pre_two):
    return pl.pallas_call(
        push_own_hidden_kernel,
        in_specs=[SMEM] + [VMEM] * 3,
        out_specs=[VMEM] * 2,
        out_shape=[
            jax.ShapeDtypeStruct((NBD + 1, FEATS, BLK), F32),
            jax.ShapeDtypeStruct((FEATS, NBD * BLK), BF16),
        ],
        compiler_params=PARAMS,
        name="push_own_hidden",
    )(tables, own, adj, pre_two)


def piece_places():
    for grad in range(2):
        for half in range(2):
            for part in range(GROUPS):
                place = (2 * grad + half) * GROUPS + part
                yield place, grad, slice(part * FEATS, (part + 1) * FEATS), slice(
                    half * BLK, (half + 1) * BLK
                )


def grads_kernel(back_two, spread_one, hidden_one, slope, weight, out):
    back = rows_of(back_two)
    along = (((1,), (1,)), ((), ()))
    carry = jnp.dot(weight[...], back, preferred_element_type=F32).astype(BF16)
    delta = (carry.astype(F32) * slope[...]).astype(BF16)
    sums = (
        lax.dot_general(rows_of(spread_one), delta, along, preferred_element_type=F32),
        lax.dot_general(rows_of(hidden_one), back, along, preferred_element_type=F32),
    )
    for place, grad, rows, columns in piece_places():
        out[place] = sums[grad][rows, columns].astype(BF16)


def grads(back_two, spread_one, hidden_one, slope, weight):
    return pl.pallas_call(
        grads_kernel,
        in_specs=[VMEM] * 5,
        out_specs=VMEM,
        out_shape=blocks_of(),
        compiler_params=PARAMS,
        name="grads",
    )(back_two, spread_one, hidden_one, slope, weight)


def finish_kernel(pieces, grad_one, grad_two):
    outs = (grad_one, grad_two)
    for place, grad, rows, columns in piece_places():
        outs[grad][rows, columns] = pieces[place].astype(F32)


def finish(pieces):
    size = GROUPS * FEATS
    return pl.pallas_call(
        finish_kernel,
        in_specs=[VMEM],
        out_specs=[VMEM] * 2,
        out_shape=[jax.ShapeDtypeStruct((size, size), F32)] * 2,
        compiler_params=PARAMS,
        name="finish",
    )(pieces)


def gather_pieces(piece, axes):
    spread = jnp.broadcast_to(piece[None], (lax.axis_size(axes),) + piece.shape)
    return exchange(spread, axes)


def sum_everywhere(partial):
    pieces = exchange(partial, PLANE).reshape(lax.axis_size(PLANE), -1, BLK)
    piece = jnp.sum(pieces.astype(F32), axis=0).astype(BF16)
    piece = jnp.sum(gather_pieces(piece, "zlo").astype(F32), axis=0).astype(BF16)
    piece = jnp.sum(gather_pieces(piece, "zhi").astype(F32), axis=0).astype(BF16)
    return gather_pieces(piece, PLANE).reshape(partial.shape)


def shards(
    features,
    weight_one,
    weight_two,
    blk_rows,
    blk_cols,
    blk_counts,
    adj_values,
    adj_tvalues,
    cotangent,
):
    base = lax.axis_index(NODE).astype(jnp.int32) * NBD
    spread = lambda scalar: jnp.broadcast_to(scalar, blk_rows.shape)
    slots = jnp.concatenate([blk_rows, blk_cols, spread(blk_counts[0]), spread(base)])
    tables, own, *sends = split_blocks(slots, features)
    spread_one = exchange(apply_blocks(tables, own, sends, adj_values), FEAT)
    hidden_rows, slope_one = mix_one(spread_one, weight_one)
    own = exchange(hidden_rows, FEAT)
    spread_two = exchange(apply_blocks(tables, own, sends_of(tables, own), adj_values), FEAT)
    pre_two = exchange(mix_two(spread_two, weight_two), FEAT)
    delta_two, *sends = turn(tables, pre_two, cotangent)
    low, high = halo(*sends)
    begun, hidden_out = push_own_hidden(tables, delta_two, adj_values, pre_two)
    back_two = exchange(apply_halo(tables, begun, low, high, adj_tvalues), FEAT)
    partial = grads(back_two, spread_one, hidden_rows, slope_one, weight_two)
    grad_one, grad_two = finish(sum_everywhere(partial))
    return (hidden_out, grad_one, grad_two)


def solution(mesh):
    fine = Mesh(np.asarray(mesh.devices).reshape(tuple(FINE.values())), tuple(FINE))
    return jax.shard_map(
        shards,
        mesh=fine,
        in_specs=(
            P(FEAT, NODE),
            P(),
            P(),
            P(NODE, None),
            P(NODE, None),
            P(NODE),
            P(NODE, None, None),
            P(NODE, None, None),
            P(FEAT, NODE),
        ),
        out_specs=(P(FEAT, NODE), P(), P()),
        check_vma=False,
    )
```
